256 devices in a mesh: az: 16 (over y_lo, z), tm: 16 (over y_hi, x, core).
Axes of the slice: x: 4, y: 4 (y_hi: 2, y_lo: 2; y = y_hi * 2 + y_lo), z: 8, core: 2. Of those that a mesh axis runs over, the one named last changes fastest.
Arguments:
- teacher_q: bfloat16 [16, 2048, 2560], P('az', 'tm'), may hold values from -6 to 6
- teacher_k: bfloat16 [16, 2048, 2560], P('az', 'tm'), may hold values from -6 to 6
- teacher_v: bfloat16 [16, 2048, 2560], P('az', 'tm'), may hold values from -96 to 96
- band: int32 [16, 16], P('tm', 'az'), may hold values from 0 to 4, as said below
- head_mix: float32 [20, 8], replicated, may hold values from -1.25 to 1.25
- latents: bfloat16 [16, 2048, 1024], P('az', 'tm'), may hold values from -6 to 6
- w_qk: bfloat16 [1024, 2048], replicated, may hold values from -0.1875 to 0.1875
- w_v: bfloat16 [1024, 1024], replicated, may hold values from -1.5 to 1.5
Outputs:
- gap: float32 [16, 2048, 1024], P('az', 'tm')
The draws below stay inside these ranges and needn't reach their ends.
Inputs may be any that keep to these rules, and one draw needn't show every extreme that they name: `band`: every time block has at least one azimuth block whose half-width is 4.
All inputs are finite; a program needn't handle non-finite values.
Results may differ from the reference program's by a relative error of at most 0.0052.
Values may be sent and summed in bfloat16 or wider, within the bound.
A program may use at most 128 MiB of HBM per device.

```python
import math
import jax
import jax.numpy as jnp
from jax import lax

HT = 20
HD = 128
DS = 1024
TOK_DEV = 128
HS = 8
AZ_BLOCKS = 16
TIME_BLOCKS = 16
TIME_TOKENS = 2048
HMAX = 4
WIN = 64


def draw_band(key, part):
    key = jax.random.fold_in(key, 1)
    base = jax.random.randint(key, (TIME_BLOCKS, AZ_BLOCKS), 0, HMAX // 2 + 1)
    picked = jax.random.randint(jax.random.fold_in(key, 2), (TIME_BLOCKS,), 0, AZ_BLOCKS)
    onehot = jnp.arange(AZ_BLOCKS)[None, :] == picked[:, None]
    return jnp.where(onehot, HMAX, base).astype(jnp.int32)


def block_scale(stream_key, shape, pieces, least, high):
    def one(position, shards_of):
        draws = jax.random.uniform(jax.random.fold_in(jax.random.fold_in(stream_key, 6), position), (shards_of,), jnp.float32, least / len(pieces), high / len(pieces))
        return jnp.repeat(jnp.exp(draws), shape[position] // shards_of).reshape((-1,) + (1,) * (len(shape) - position - 1))

    factor_of = one(*pieces[0])
    for cut in pieces[1:]:
        factor_of = factor_of * one(*cut)
    return factor_of


def scatter_about(stream_key, shape, scale, bound, split=(), held_as=jnp.bfloat16):
    loudness = block_scale(stream_key, shape, split, -0.22, 0.18) if split else 1.0
    entries = jax.random.normal(stream_key, shape, jnp.float32) * scale * loudness
    return jnp.minimum(jnp.maximum(entries, -bound), bound).astype(held_as)


def setup_inputs(seed: int = 0) -> dict:
    streams_of = jax.random.split(jax.random.key(seed), 9)
    return {
        "teacher_q": scatter_about(streams_of[0], (AZ_BLOCKS, TIME_TOKENS, HT * HD), 1.0, 6.0, ((0, 16), (1, 16))),
        "teacher_k": scatter_about(streams_of[1], (AZ_BLOCKS, TIME_TOKENS, HT * HD), 1.0, 6.0, ((0, 16), (1, 16))),
        "teacher_v": scatter_about(streams_of[2], (AZ_BLOCKS, TIME_TOKENS, HT * HD), 16.0, 96.0, ((0, 16), (1, 16))),
        "band": draw_band(jax.random.fold_in(streams_of[8], 71), 0),
        "head_mix": scatter_about(streams_of[4], (HT, HS), HT ** -0.5, 1.25, (), jnp.float32),
        "latents": scatter_about(streams_of[5], (AZ_BLOCKS, TIME_TOKENS, DS), 1.0, 6.0, ((0, 16), (1, 16))),
        "w_qk": scatter_about(streams_of[6], (DS, 2 * DS), DS ** -0.5, 0.1875),
        "w_v": scatter_about(streams_of[7], (DS, DS), 0.25, 1.5),
    }


def headnorm(u, heads):
    shaped = u.reshape(u.shape[:-1] + (heads, u.shape[-1] // heads))
    return shaped * lax.rsqrt(lax.optimization_barrier(jnp.mean(shaped * shaped, axis=-1, keepdims=True)) + 1e-06)

def reference(teacher_q, teacher_k, teacher_v, band, head_mix, latents, w_qk, w_v):
    scale = 1.0 / math.sqrt(HD)
    tq = headnorm(teacher_q.astype(jnp.float32), HT).astype(jnp.bfloat16)
    tk = headnorm(teacher_k.astype(jnp.float32), HT).astype(jnp.bfloat16)
    tq = tq.reshape(AZ_BLOCKS, TIME_BLOCKS, TOK_DEV, HT, HD)
    tk = tk.reshape(AZ_BLOCKS, TIME_BLOCKS, TOK_DEV, HT, HD)
    tv = teacher_v.reshape(AZ_BLOCKS, TIME_BLOCKS, TOK_DEV, HT, HD)

    def teacher_one(block):
        queries = tq[block].astype(jnp.float32)
        total = jnp.zeros((TIME_BLOCKS, HT, TOK_DEV), jnp.float32)
        accum = jnp.zeros((TIME_BLOCKS, HT, TOK_DEV, HD), jnp.float32)
        for offset in range(-HMAX, HMAX + 1):
            other = (block + offset) % AZ_BLOCKS
            keys = tk[other].astype(jnp.float32)
            values = tv[other].astype(jnp.float32)
            scores = jnp.einsum('tqhd,tkhd->thqk', queries, keys) * scale
            keep = abs(offset) <= band[:, block]
            probs = jnp.where(keep[:, None, None, None], jnp.exp(scores), 0.0)
            total = total + lax.optimization_barrier(jnp.sum(probs, axis=-1))
            accum = accum + jnp.einsum('thqk,tkhd->thqd', probs.astype(jnp.bfloat16).astype(jnp.float32), values)
        tout = accum / total[..., None]
        mixed = jnp.einsum('thqd,hs->tqsd', tout, head_mix, precision=lax.Precision.HIGHEST)
        return mixed.reshape(TIME_TOKENS, DS)

    def student_one(block):
        rows = latents[block]
        qk = jnp.dot(rows, w_qk, preferred_element_type=jnp.float32)
        sv = jnp.dot(rows, w_v, preferred_element_type=jnp.float32)
        snq = headnorm(qk[:, :DS], HS).astype(jnp.bfloat16)
        snk = headnorm(qk[:, DS:], HS).astype(jnp.bfloat16)
        svr = sv.astype(jnp.bfloat16).reshape(TIME_TOKENS, HS, HD)
        padded_k = jnp.pad(snk, ((WIN, WIN), (0, 0), (0, 0)))
        padded_v = jnp.pad(svr, ((WIN, WIN), (0, 0), (0, 0)))

        def time_one(tblock):
            start = (tblock * TOK_DEV).astype(jnp.int32)
            queries = lax.dynamic_slice_in_dim(snq, start, TOK_DEV, 0).astype(jnp.float32)
            keys = lax.dynamic_slice_in_dim(padded_k, start, TOK_DEV + 2 * WIN, 0).astype(jnp.float32)
            values = lax.dynamic_slice_in_dim(padded_v, start, TOK_DEV + 2 * WIN, 0).astype(jnp.float32)
            scores = jnp.einsum('qhd,khd->hqk', queries, keys) * scale
            pos_q = start + jnp.arange(TOK_DEV, dtype=jnp.int32)[:, None]
            pos_k = start - WIN + jnp.arange(TOK_DEV + 2 * WIN, dtype=jnp.int32)[None, :]
            keep = (jnp.abs(pos_q - pos_k) <= WIN) & (pos_k >= 0) & (pos_k < TIME_TOKENS)
            probs = jnp.where(keep[None], jnp.exp(scores), 0.0)
            total = lax.optimization_barrier(jnp.sum(probs, axis=-1))
            accum = jnp.einsum('hqk,khd->hqd', probs.astype(jnp.bfloat16).astype(jnp.float32), values)
            sout = accum / total[..., None]
            return jnp.transpose(sout, (1, 0, 2)).reshape(TOK_DEV, DS)
        outs = lax.map(time_one, jnp.arange(TIME_BLOCKS, dtype=jnp.int32))
        return outs.reshape(TIME_TOKENS, DS)

    def both(block):
        return student_one(block) - teacher_one(block)
    return lax.map(both, jnp.arange(AZ_BLOCKS, dtype=jnp.int32))
```

```python
import math

import jax
import jax.numpy as jnp
from jax import lax
from jax.experimental import pallas as pl
from jax.experimental.pallas import tpu as pltpu
from jax.sharding import PartitionSpec as P

MESH = pl.DeviceIdType.MESH
BF = jnp.bfloat16
F32 = jnp.float32
REACH = 4
CH = 2
HALVES = 2
LANES = 128


def normed(x):
    return x * lax.rsqrt(jnp.mean(x * x, axis=-1, keepdims=True) + 1e-06)


def kernel(
    q_hbm, k_hbm, v_hbm, band_ref, mix_ref, lat_hbm, wqk_hbm, wv_hbm, out_hbm,
    q_in, k_in, v_in, lat, wqk, wv,
    qn, kt, qbuf, o_ref, pp, tsnd, tbuf, rsnd, rbuf, msnd, mbuf, town, sout, outv,
    in_sem, out_sem, lat_s, lat_r, q_s, q_r, t_s, t_r, r_s, r_r, m_s, m_r,
):
    az = lax.axis_index("az")
    tm = lax.axis_index("tm")
    n_az = lax.axis_size("az")
    n_tm = lax.axis_size("tm")
    heads_t, heads_s = mix_ref.shape
    rows, tokens = qn.shape[2], q_in.shape[0]
    hd = LANES
    per_half = heads_t // HALVES
    scale2 = math.log2(math.e) / math.sqrt(hd)

    def az_dev(by):
        return (lax.rem(az + by + n_az, n_az), tm)

    def tm_dev(by):
        return (az, lax.rem(tm + by + n_tm, n_tm))

    window = tokens // 2
    loads = [
        pltpu.make_async_copy(q_hbm.at[0], q_in, in_sem.at[0]),
        pltpu.make_async_copy(k_hbm.at[0], k_in, in_sem.at[1]),
        pltpu.make_async_copy(lat_hbm.at[0], lat.at[pl.ds(window, tokens)], in_sem.at[2]),
        pltpu.make_async_copy(v_hbm.at[0], v_in, in_sem.at[3]),
        pltpu.make_async_copy(wqk_hbm, wqk, in_sem.at[4]),
        pltpu.make_async_copy(wv_hbm, wv, in_sem.at[5]),
    ]
    for load in loads:
        load.start()

    barrier = pltpu.get_barrier_semaphore()
    for d in range(1, REACH + 1):
        for sign in (1, -1):
            pl.semaphore_signal(barrier, inc=1, device_id=az_dev(sign * d), device_id_type=MESH)
    for sign in (1, -1):
        pl.semaphore_signal(barrier, inc=1, device_id=tm_dev(sign), device_id_type=MESH)

    def remote(src, dst, send, recv, dev):
        return pltpu.make_async_remote_copy(
            src_ref=src, dst_ref=dst, send_sem=send, recv_sem=recv, device_id=dev, device_id_type=MESH
        )

    def q_copy(side, c, k, half):
        part = pl.ds(half * per_half, per_half)
        src = qn.at[c, part] if isinstance(k, int) and k == 1 else qbuf.at[side, c, k - 2, part]
        return remote(
            src, qbuf.at[side, c, k - 1, part],
            q_s.at[side, c, k - 1, half], q_r.at[side, c, k - 1, half], az_dev(1 - 2 * side),
        )

    def t_copy(side, c, k):
        return remote(
            tsnd.at[side, c, k - 1], tbuf.at[side, c, k - 1],
            t_s.at[side, c, k - 1], t_r.at[side, c, k - 1], az_dev((2 * side - 1) * k),
        )

    def r_copy(side, c, k):
        return remote(
            rsnd.at[c, k - 1], rbuf.at[side, c, k - 1],
            r_s.at[side, c, k - 1], r_r.at[side, c, k - 1], az_dev((1 - 2 * side) * k),
        )

    def m_copy(side, c, k):
        return remote(
            msnd.at[side, c, k - 1], mbuf.at[side, c, k - 1],
            m_s.at[side, c, k - 1], m_r.at[side, c, k - 1], az_dev(2 * side - 1),
        )

    def lat_copy(side):
        src = lat.at[pl.ds(window + (1 - side) * (tokens - window), window)]
        dst = lat.at[pl.ds(side * (tokens + window), window)]
        return remote(src, dst, lat_s.at[side], lat_r.at[side], tm_dev(1 - 2 * side))

    def norm_q(c, half):
        def one(i, _):
            h = half * per_half + i
            x = q_in[c * rows:(c + 1) * rows, pl.ds(pl.multiple_of(h * hd, hd), hd)].astype(F32)
            qn[c, h] = normed(x).astype(BF)
            return 0
        lax.fori_loop(0, per_half, one, 0, unroll=5)

    loads[0].wait()
    norm_q(0, 0)
    pl.semaphore_wait(barrier, 2 * REACH + 2)
    for side in (0, 1):
        q_copy(side, 0, 1, 0).start()
    norm_q(0, 1)
    for side in (0, 1):
        q_copy(side, 0, 1, 1).start()
    loads[2].wait()
    for side in (0, 1):
        lat_copy(side).start()
    norm_q(1, 0)
    norm_q(1, 1)

    loads[1].wait()

    def norm_k(h, _):
        x = k_in[:, pl.ds(pl.multiple_of(h * hd, hd), hd)].astype(F32)
        kt[h] = normed(x).T.astype(BF)
        return 0

    lax.fori_loop(0, heads_t, norm_k, 0, unroll=4)
    loads[3].wait()

    lane = lax.broadcasted_iota(jnp.int32, (tokens, LANES), 1)
    lane8 = lax.broadcasted_iota(jnp.int32, (8, LANES), 1)

    def scores(left, right, idx, half, sums):
        def group(i, sums):
            for j in range(5):
                h = half * per_half + i * 5 + j
                q = jnp.concatenate([left[h], right[h]], axis=0)
                s = jnp.dot(q, kt[h], preferred_element_type=F32)
                p = jnp.exp2(s * scale2)
                sums = jnp.where(lane == h, jnp.sum(p, axis=1, keepdims=True), sums)
                v = v_in[:, pl.ds(pl.multiple_of(h * hd, hd), hd)]
                o_ref[idx, h] = jnp.dot(p.astype(BF), v, preferred_element_type=F32)
            return sums
        return lax.fori_loop(0, per_half // 5, group, sums)

    half_lanes = LANES // 2

    def swap(x):
        return pltpu.roll(x, half_lanes, 1)

    def pick(x, y):
        return jnp.where(lane8 < half_lanes, x, y)

    def pack(sums):
        t = sums.T
        t0, t1, t2 = t[0:8], t[8:16], t[16:24]
        low = jnp.concatenate([pick(t0, swap(t1)), t2], axis=0)
        high = jnp.concatenate([pick(swap(t0), t1), swap(t2)], axis=0)
        return low, high

    def unpack(low, high):
        t0 = pick(low[0:8], swap(high[0:8]))
        t1 = pick(swap(low[0:8]), high[0:8])
        t2 = pick(low[8:16], swap(high[8:16]))
        return jnp.concatenate([t0, t1, t2, jnp.zeros((LANES - 24, LANES), F32)], axis=0).T

    zeros = jnp.zeros((tokens, LANES), F32)

    def own_scores():
        sums = scores(qn.at[0], qn.at[1], CH * REACH, 0, zeros)
        sums = scores(qn.at[0], qn.at[1], CH * REACH, 1, sums)
        low, high = pack(sums)
        town[0] = low
        town[1] = high

    def send_sums(c, k, sums):
        for side, t in enumerate(pack(sums)):
            tsnd[side, c, k - 1] = t.astype(BF)
            t_copy(side, c, k).start()

    def gather_sums(c):
        reach = band_ref[0, 0]
        total = town[c]
        keeps = []
        for k in range(1, REACH + 1):
            keep = jnp.where(k <= reach, 1.0, 0.0).astype(F32)
            keeps.append(keep)
            for side in (0, 1):
                t_copy(side, c, k).wait_recv()
                total = total + keep * tbuf[side, c, k - 1].astype(F32)
        inverse = 1.0 / total
        town[c] = inverse
        for k in range(1, REACH + 1):
            rsnd[c, k - 1] = (keeps[k - 1] * inverse).astype(BF)
            for side in (0, 1):
                r_copy(side, c, k).start()

    block = 32

    def mix_tile(idx, factors):
        fac_rows = factors
        town[2:] = fac_rows.reshape(tokens // 16, 16, LANES)

        def one(b, _):
            at = pl.multiple_of(b * block, block)
            f = town[pl.ds(2 + b * (block // 16), block // 16)].reshape(block, LANES)
            acc = [None] * heads_s
            for h in range(heads_t):
                x = o_ref[idx, h, pl.ds(at, block)] * f[:, h:h + 1]
                for s in range(heads_s):
                    y = x * mix_ref[h, s]
                    acc[s] = y if acc[s] is None else acc[s] + y
            for s in range(heads_s):
                pp[idx, pl.ds(at, block), s * hd:(s + 1) * hd] = acc[s]
            return 0
        lax.fori_loop(0, tokens // block, one, 0)

    def mix_remote(c, k):
        for side in (0, 1):
            r_copy(side, c, k).wait_recv()
        mix_tile(c * REACH + k - 1, unpack(rbuf[0, c, k - 1].astype(F32), rbuf[1, c, k - 1].astype(F32)))

    def pass_back(c, k):
        for side in (0, 1):
            part = pp[c * REACH + k - 1, side * rows:(side + 1) * rows]
            if k < REACH:
                m_copy(side, c, k + 1).wait_recv()
                part = part + mbuf[side, c, k].astype(F32)
            msnd[side, c, k - 1] = part.astype(BF)
            m_copy(side, c, k).start()

    span = tokens + 2 * window

    def student(pair):
        cols = 2 * hd
        at = pl.multiple_of(pair * cols, cols)
        width = heads_s * hd
        sq = jnp.dot(lat[pl.ds(window, tokens)], wqk[:, pl.ds(at, cols)], preferred_element_type=F32)
        sk = jnp.dot(lat[...], wqk[:, pl.ds(pl.multiple_of(width + pair * cols, cols), cols)], preferred_element_type=F32)
        sv = jnp.dot(lat[...], wv[:, pl.ds(at, cols)], preferred_element_type=F32).astype(BF)
        pos_q = lax.broadcasted_iota(jnp.int32, (tokens, span), 0)
        pos_k = lax.broadcasted_iota(jnp.int32, (tokens, span), 1) - window
        at_k = pos_k + tm * tokens
        keep = (jnp.abs(pos_q - pos_k) <= window) & (at_k >= 0) & (at_k < n_tm * tokens)
        for j in range(2):
            part = slice(j * hd, (j + 1) * hd)
            snq = normed(sq[:, part]).astype(BF)
            snk = normed(sk[:, part]).astype(BF)
            s = lax.dot_general(snq, snk, (((1,), (1,)), ((), ())), preferred_element_type=F32)
            p = jnp.where(keep, jnp.exp2(s * scale2), 0.0)
            total = jnp.sum(p, axis=1, keepdims=True)
            o = jnp.dot(p.astype(BF), sv[:, part], preferred_element_type=F32)
            sout[:, pl.ds(pl.multiple_of(at + j * hd, hd), hd)] = o / total

    def arrive(c, k, half, sums):
        for side in (0, 1):
            q_copy(side, c, k, half).wait_recv()
            if k < REACH:
                q_copy(side, c, k + 1, half).start()
            elif c + 1 < CH:
                q_copy(side, c + 1, 1, half).start()
        return scores(qbuf.at[0, c, k - 1], qbuf.at[1, c, k - 1], c * REACH + k - 1, half, sums)

    for k in range(1, REACH + 1):
        sums = arrive(0, k, 0, zeros)
        if k == 1:
            own_scores()
        if k == 2:
            loads[4].wait()
            loads[5].wait()
            for side in (0, 1):
                lat_copy(side).wait_recv()
        if k >= 2:
            student(k - 2)
        sums = arrive(0, k, 1, sums)
        send_sums(0, k, sums)

    for k in range(1, REACH + 1):
        sums = arrive(1, k, 0, zeros)
        if k == 1:
            student(3)
        if k == 2:
            gather_sums(0)
        if k == 4:
            mix_remote(0, 4)
            pass_back(0, 4)
        sums = arrive(1, k, 1, sums)
        send_sums(1, k, sums)
    mix_remote(0, 3)
    pass_back(0, 3)
    gather_sums(1)
    mix_remote(0, 2)
    pass_back(0, 2)
    mix_remote(1, 4)
    pass_back(1, 4)
    mix_remote(0, 1)
    pass_back(0, 1)
    mix_remote(1, 3)
    pass_back(1, 3)
    mix_remote(1, 2)
    mix_remote(1, 1)
    pass_back(1, 2)
    low, high = town[0], town[1]
    mix_tile(CH * REACH, unpack(low, high))
    pass_back(1, 1)

    for c in range(CH):
        target = pp[CH * REACH, c * rows:(c + 1) * rows]
        for side in (0, 1):
            m_copy(side, c, 1).wait_recv()
            target = target + mbuf[side, c, 0].astype(F32)
        outv[c * rows:(c + 1) * rows] = sout[c * rows:(c + 1) * rows] - target
        pltpu.make_async_copy(
            outv.at[pl.ds(c * rows, rows)], out_hbm.at[0, pl.ds(c * rows, rows)], out_sem.at[c]
        ).start()

    for side in (0, 1):
        lat_copy(side).wait_send()
        for c in range(CH):
            for k in range(1, REACH + 1):
                for half in range(HALVES):
                    q_copy(side, c, k, half).wait_send()
                t_copy(side, c, k).wait_send()
                r_copy(side, c, k).wait_send()
                m_copy(side, c, k).wait_send()
    for c in range(CH):
        pltpu.make_async_copy(
            outv.at[pl.ds(c * rows, rows)], out_hbm.at[0, pl.ds(c * rows, rows)], out_sem.at[c]
        ).wait()


def shards(teacher_q, teacher_k, teacher_v, band, head_mix, latents, w_qk, w_v):
    tokens, width = teacher_q.shape[1:]
    heads_t, heads_s = head_mix.shape
    hd = width // heads_t
    student_width = latents.shape[2]
    rows = tokens // CH
    tiles = CH * REACH
    dma = pltpu.SemaphoreType.DMA
    anywhere = pl.BlockSpec(memory_space=pl.ANY)
    scalars = pl.BlockSpec(memory_space=pltpu.SMEM)
    return pl.pallas_call(
        kernel,
        out_shape=jax.ShapeDtypeStruct((1, tokens, student_width), F32),
        in_specs=[anywhere, anywhere, anywhere, scalars, scalars, anywhere, anywhere, anywhere],
        out_specs=anywhere,
        scratch_shapes=[
            pltpu.VMEM((tokens, width), BF),
            pltpu.VMEM((tokens, width), BF),
            pltpu.VMEM((tokens, width), BF),
            pltpu.VMEM((2 * tokens, student_width), BF),
            pltpu.VMEM(w_qk.shape, BF),
            pltpu.VMEM(w_v.shape, BF),
            pltpu.VMEM((CH, heads_t, rows, hd), BF),
            pltpu.VMEM((heads_t, hd, tokens), BF),
            pltpu.VMEM((2, CH, REACH, heads_t, rows, hd), BF),
            pltpu.VMEM((tiles + 1, heads_t, tokens, hd), F32),
            pltpu.VMEM((tiles + 1, tokens, student_width), F32),
            pltpu.VMEM((2, CH, REACH, 16, LANES), BF),
            pltpu.VMEM((2, CH, REACH, 16, LANES), BF),
            pltpu.VMEM((CH, REACH, 16, LANES), BF),
            pltpu.VMEM((2, CH, REACH, 16, LANES), BF),
            pltpu.VMEM((2, CH, REACH, rows, student_width), BF),
            pltpu.VMEM((2, CH, REACH, rows, student_width), BF),
            pltpu.VMEM((2 + tokens // 16, 16, LANES), F32),
            pltpu.VMEM((tokens, student_width), F32),
            pltpu.VMEM((tokens, student_width), F32),
            dma((6,)),
            dma((CH,)),
            dma((2,)),
            dma((2,)),
            dma((2, CH, REACH, HALVES)),
            dma((2, CH, REACH, HALVES)),
            dma((2, CH, REACH)),
            dma((2, CH, REACH)),
            dma((2, CH, REACH)),
            dma((2, CH, REACH)),
            dma((2, CH, REACH)),
            dma((2, CH, REACH)),
        ],
        compiler_params=pltpu.CompilerParams(
            collective_id=0, has_side_effects=True, vmem_limit_bytes=58 * 2**20
        ),
        cost_estimate=pl.CostEstimate(flops=2 * 10**9, bytes_accessed=10**7, transcendentals=3 * 10**6),
        name="banded_teacher",
    )(teacher_q, teacher_k, teacher_v, band, head_mix, latents, w_qk, w_v)


def solution(mesh):
    in_specs = (
        P("az", "tm", None),
        P("az", "tm", None),
        P("az", "tm", None),
        P("tm", "az"),
        P(),
        P("az", "tm", None),
        P(),
        P(),
    )
    out_specs = P("az", "tm", None)
    return jax.shard_map(shards, mesh=mesh, in_specs=in_specs, out_specs=out_specs, check_vma=False)
```

```python
import math

import jax
import jax.numpy as jnp
from jax import lax
from jax.experimental import pallas as pl
from jax.experimental.pallas import tpu as pltpu
from jax.sharding import PartitionSpec as P

MESH = pl.DeviceIdType.MESH
BF = jnp.bfloat16
F32 = jnp.float32
REACH = 4
CH = 2
PIECES = 2
HALVES = 2
LANES = 128


def normed(x):
    return x * lax.rsqrt(jnp.mean(x * x, axis=-1, keepdims=True) + 1e-06)


def kernel(
    q_hbm, k_hbm, v_hbm, band_ref, mix_ref, lat_hbm, wqk_hbm, wv_hbm, out_ref,
    q_in, k_in, v_in, lat, wqk, wv,
    qn, kt, qbuf, o_ref, pp, tsnd, tbuf, rsnd, rbuf, msnd, mbuf, town, sout,
    in_sem, lat_s, lat_r, q_s, q_r, t_s, t_r, r_s, r_r, m_s, m_r,
):
    az = lax.axis_index("az")
    tm = lax.axis_index("tm")
    n_az = lax.axis_size("az")
    n_tm = lax.axis_size("tm")
    heads_s, heads_t = mix_ref.shape
    rows, tokens = qn.shape[2], q_in.shape[0]
    hd = LANES
    per_half = heads_t // HALVES
    scale2 = math.log2(math.e) / math.sqrt(hd)

    def az_dev(by):
        return (lax.rem(az + by + n_az, n_az), tm)

    def tm_dev(by):
        return (az, lax.rem(tm + by + n_tm, n_tm))

    window = tokens // 2
    first = pl.ds(0, rows)
    rest = pl.ds(rows, tokens - rows)
    loads = [
        pltpu.make_async_copy(q_hbm.at[0, first], q_in.at[first], in_sem.at[0]),
        pltpu.make_async_copy(k_hbm.at[0], k_in, in_sem.at[1]),
        pltpu.make_async_copy(lat_hbm.at[0], lat.at[pl.ds(window, tokens)], in_sem.at[2]),
        pltpu.make_async_copy(v_hbm.at[0], v_in, in_sem.at[3]),
        pltpu.make_async_copy(wqk_hbm, wqk, in_sem.at[4]),
        pltpu.make_async_copy(wv_hbm, wv, in_sem.at[5]),
        pltpu.make_async_copy(q_hbm.at[0, rest], q_in.at[rest], in_sem.at[6]),
    ]
    loads[0].start()

    barrier = pltpu.get_barrier_semaphore()
    for sign in (1, -1):
        pl.semaphore_signal(barrier, inc=1, device_id=az_dev(sign), device_id_type=MESH)
    for sign in (1, -1):
        pl.semaphore_signal(barrier, inc=1, device_id=tm_dev(sign), device_id_type=MESH)

    def remote(src, dst, send, recv, dev):
        return pltpu.make_async_remote_copy(
            src_ref=src, dst_ref=dst, send_sem=send, recv_sem=recv, device_id=dev, device_id_type=MESH
        )

    def q_copy(side, c, k, half):
        part = pl.ds(half * per_half, per_half)
        src = qn.at[c, part] if isinstance(k, int) and k == 1 else qbuf.at[side, c, k - 2, part]
        return remote(
            src, qbuf.at[side, c, k - 1, part],
            q_s.at[side, c, k - 1, half], q_r.at[side, c, k - 1, half], az_dev(1 - 2 * side),
        )

    def t_copy(side, c, k):
        return remote(
            tsnd.at[side, c, k - 1], tbuf.at[side, c, k - 1],
            t_s.at[side, c, k - 1], t_r.at[side, c, k - 1], az_dev((2 * side - 1) * k),
        )

    def r_copy(side, c, k):
        return remote(
            rsnd.at[c, k - 1], rbuf.at[side, c, k - 1],
            r_s.at[side, c, k - 1], r_r.at[side, c, k - 1], az_dev((1 - 2 * side) * k),
        )

    piece = rows // PIECES

    def m_copy(side, c, k, i):
        part = pl.ds(i * piece, piece)
        return remote(
            msnd.at[side, c, k - 1, part], mbuf.at[side, c, k - 1, part],
            m_s.at[side, c, k - 1, i], m_r.at[side, c, k - 1, i], az_dev(2 * side - 1),
        )

    def lat_copy(side):
        src = lat.at[pl.ds(window + (1 - side) * (tokens - window), window)]
        dst = lat.at[pl.ds(side * (tokens + window), window)]
        return remote(src, dst, lat_s.at[side], lat_r.at[side], tm_dev(1 - 2 * side))

    def norm_q(c, half):
        def one(i, _):
            h = half * per_half + i
            x = q_in[c * rows:(c + 1) * rows, pl.ds(pl.multiple_of(h * hd, hd), hd)].astype(F32)
            qn[c, h] = normed(x).astype(BF)
            return 0
        lax.fori_loop(0, per_half, one, 0, unroll=5)

    loads[0].wait()
    for i in (1, 2, 6, 3, 4, 5):
        loads[i].start()
    norm_q(0, 0)
    pl.semaphore_wait(barrier, 4)
    for side in (0, 1):
        q_copy(side, 0, 1, 0).start()
    norm_q(0, 1)
    for side in (0, 1):
        q_copy(side, 0, 1, 1).start()
    loads[2].wait()
    for side in (0, 1):
        lat_copy(side).start()
    loads[1].wait()

    def norm_k(h, _):
        x = k_in[:, pl.ds(pl.multiple_of(h * hd, hd), hd)].astype(F32)
        kt[h] = normed(x).T.astype(BF)
        return 0

    lax.fori_loop(0, heads_t, norm_k, 0, unroll=4)
    loads[6].wait()
    norm_q(1, 0)
    norm_q(1, 1)
    loads[3].wait()

    lane = lax.broadcasted_iota(jnp.int32, (tokens, LANES), 1)
    lane8 = lax.broadcasted_iota(jnp.int32, (8, LANES), 1)

    def scores(left, right, idx, half, sums):
        def group(i, sums):
            for j in range(5):
                h = half * per_half + i * 5 + j
                q = jnp.concatenate([left[h], right[h]], axis=0)
                s = jnp.dot(q, kt[h], preferred_element_type=F32)
                p = jnp.exp2(s * scale2)
                sums = jnp.where(lane == h, jnp.sum(p, axis=1, keepdims=True), sums)
                v = v_in[:, pl.ds(pl.multiple_of(h * hd, hd), hd)]
                o_ref[idx, h] = jnp.dot(p.astype(BF), v, preferred_element_type=F32)
            return sums
        return lax.fori_loop(0, per_half // 5, group, sums)

    half_lanes = LANES // 2

    def swap(x):
        return pltpu.roll(x, half_lanes, 1)

    def pick(x, y):
        return jnp.where(lane8 < half_lanes, x, y)

    def pack(sums):
        t = sums.T
        t0, t1, t2 = t[0:8], t[8:16], t[16:24]
        low = jnp.concatenate([pick(t0, swap(t1)), t2], axis=0)
        high = jnp.concatenate([pick(swap(t0), t1), swap(t2)], axis=0)
        return low, high

    def unpack(low, high):
        t0 = pick(low[0:8], swap(high[0:8]))
        t1 = pick(swap(low[0:8]), high[0:8])
        t2 = pick(low[8:16], swap(high[8:16]))
        return jnp.concatenate([t0, t1, t2, jnp.zeros((LANES - 24, LANES), F32)], axis=0).T

    zeros = jnp.zeros((tokens, LANES), F32)

    def own_scores():
        sums = scores(qn.at[0], qn.at[1], CH * REACH, 0, zeros)
        sums = scores(qn.at[0], qn.at[1], CH * REACH, 1, sums)
        low, high = pack(sums)
        town[0] = low
        town[1] = high

    def send_sums(c, k, sums):
        for side, t in enumerate(pack(sums)):
            tsnd[side, c, k - 1] = t.astype(BF)
            t_copy(side, c, k).start()

    def gather_sums(c):
        reach = band_ref[0, 0]
        total = town[c]
        keeps = []
        for k in range(1, REACH + 1):
            keep = jnp.where(k <= reach, 1.0, 0.0).astype(F32)
            keeps.append(keep)
            for side in (0, 1):
                t_copy(side, c, k).wait_recv()
                total = total + keep * tbuf[side, c, k - 1].astype(F32)
        inverse = 1.0 / total
        town[c] = inverse
        for k in range(1, REACH + 1):
            rsnd[c, k - 1] = (keeps[k - 1] * inverse).astype(BF)
            for side in (0, 1):
                r_copy(side, c, k).start()

    block = 32

    def mix_tile(idx, factors):
        fac_rows = factors
        town[2:] = fac_rows.reshape(tokens // 16, 16, LANES)

        def one(b, _):
            at = pl.multiple_of(b * block, block)
            f = town[pl.ds(2 + b * (block // 16), block // 16)].reshape(block, LANES)
            acc = [None] * heads_s
            for h in range(heads_t):
                x = o_ref[idx, h, pl.ds(at, block)] * f[:, h:h + 1]
                for s in range(heads_s):
                    y = x * mix_ref[s, h]
                    acc[s] = y if acc[s] is None else acc[s] + y
            for s in range(heads_s):
                pp[idx, pl.ds(at, block), s * hd:(s + 1) * hd] = acc[s]
            return 0
        lax.fori_loop(0, tokens // block, one, 0)

    def mix_remote(c, k):
        for side in (0, 1):
            r_copy(side, c, k).wait_recv()
        mix_tile(c * REACH + k - 1, unpack(rbuf[0, c, k - 1].astype(F32), rbuf[1, c, k - 1].astype(F32)))

    def pass_back(c, k):
        for i in range(PIECES):
            at = slice(i * piece, (i + 1) * piece)
            for side in (0, 1):
                part = pp[c * REACH + k - 1, side * rows + i * piece:side * rows + (i + 1) * piece]
                if k < REACH:
                    m_copy(side, c, k + 1, i).wait_recv()
                    part = part + mbuf[side, c, k, at].astype(F32)
                msnd[side, c, k - 1, at] = part.astype(BF)
                m_copy(side, c, k, i).start()

    span = tokens + 2 * window

    def student(pair):
        cols = 2 * hd
        at = pl.multiple_of(pair * cols, cols)
        width = heads_s * hd
        sq = jnp.dot(lat[pl.ds(window, tokens)], wqk[:, pl.ds(at, cols)], preferred_element_type=F32)
        sk = jnp.dot(lat[...], wqk[:, pl.ds(pl.multiple_of(width + pair * cols, cols), cols)], preferred_element_type=F32)
        sv = jnp.dot(lat[...], wv[:, pl.ds(at, cols)], preferred_element_type=F32).astype(BF)
        pos_q = lax.broadcasted_iota(jnp.int32, (tokens, span), 0)
        pos_k = lax.broadcasted_iota(jnp.int32, (tokens, span), 1) - window
        at_k = pos_k + tm * tokens
        keep = (jnp.abs(pos_q - pos_k) <= window) & (at_k >= 0) & (at_k < n_tm * tokens)
        for j in range(2):
            part = slice(j * hd, (j + 1) * hd)
            snq = normed(sq[:, part]).astype(BF)
            snk = normed(sk[:, part]).astype(BF)
            s = lax.dot_general(snq, snk, (((1,), (1,)), ((), ())), preferred_element_type=F32)
            p = jnp.where(keep, jnp.exp2(s * scale2), 0.0)
            total = jnp.sum(p, axis=1, keepdims=True)
            o = jnp.dot(p.astype(BF), sv[:, part], preferred_element_type=F32)
            sout[:, pl.ds(pl.multiple_of(at + j * hd, hd), hd)] = o / total

    def arrive(c, k, half, sums):
        for side in (0, 1):
            q_copy(side, c, k, half).wait_recv()
            if k < REACH:
                q_copy(side, c, k + 1, half).start()
            elif c + 1 < CH:
                q_copy(side, c + 1, 1, half).start()
        return scores(qbuf.at[0, c, k - 1], qbuf.at[1, c, k - 1], c * REACH + k - 1, half, sums)

    for k in range(1, REACH + 1):
        sums = arrive(0, k, 0, zeros)
        if k == 1:
            own_scores()
        if k == 2:
            loads[4].wait()
            loads[5].wait()
            for side in (0, 1):
                lat_copy(side).wait_recv()
        if k >= 2:
            student(k - 2)
        sums = arrive(0, k, 1, sums)
        send_sums(0, k, sums)

    for k in range(1, REACH + 1):
        sums = arrive(1, k, 0, zeros)
        if k == 1:
            student(3)
        if k == 2:
            gather_sums(0)
        if k == 3:
            mix_remote(0, 4)
        if k == 4:
            pass_back(0, 4)
            mix_remote(0, 2)
        sums = arrive(1, k, 1, sums)
        send_sums(1, k, sums)
        if k == 3:
            mix_remote(0, 3)
    pass_back(0, 3)
    mix_remote(0, 1)
    pass_back(0, 2)
    gather_sums(1)
    pass_back(0, 1)
    mix_tile(CH * REACH, unpack(town[0], town[1]))
    for k in range(REACH, 0, -1):
        mix_remote(1, k)
        pass_back(1, k)

    for c in range(CH):
        for i in range(PIECES):
            at = slice(c * rows + i * piece, c * rows + (i + 1) * piece)
            target = pp[CH * REACH, at]
            for side in (0, 1):
                m_copy(side, c, 1, i).wait_recv()
                target = target + mbuf[side, c, 0, i * piece:(i + 1) * piece].astype(F32)
            out_ref[0, at] = sout[at] - target

    for side in (0, 1):
        lat_copy(side).wait_send()
        for c in range(CH):
            for k in range(1, REACH + 1):
                for half in range(HALVES):
                    q_copy(side, c, k, half).wait_send()
                t_copy(side, c, k).wait_send()
                r_copy(side, c, k).wait_send()
                for i in range(PIECES):
                    m_copy(side, c, k, i).wait_send()


def shards(teacher_q, teacher_k, teacher_v, band, head_mix, latents, w_qk, w_v):
    tokens, width = teacher_q.shape[1:]
    heads_t, heads_s = head_mix.shape
    hd = width // heads_t
    student_width = latents.shape[2]
    rows = tokens // CH
    tiles = CH * REACH
    dma = pltpu.SemaphoreType.DMA
    anywhere = pl.BlockSpec(memory_space=pl.ANY)
    scalars = pl.BlockSpec(memory_space=pltpu.SMEM)
    return pl.pallas_call(
        kernel,
        out_shape=pltpu.VMEM((1, tokens, student_width), F32),
        in_specs=[anywhere, anywhere, anywhere, scalars, scalars, anywhere, anywhere, anywhere],
        out_specs=pl.BlockSpec(memory_space=pltpu.VMEM),
        scratch_shapes=[
            pltpu.VMEM((tokens, width), BF),
            pltpu.VMEM((tokens, width), BF),
            pltpu.VMEM((tokens, width), BF),
            pltpu.VMEM((2 * tokens, student_width), BF),
            pltpu.VMEM(w_qk.shape, BF),
            pltpu.VMEM(w_v.shape, BF),
            pltpu.VMEM((CH, heads_t, rows, hd), BF),
            pltpu.VMEM((heads_t, hd, tokens), BF),
            pltpu.VMEM((2, CH, REACH, heads_t, rows, hd), BF),
            pltpu.VMEM((tiles + 1, heads_t, tokens, hd), F32),
            pltpu.VMEM((tiles + 1, tokens, student_width), F32),
            pltpu.VMEM((2, CH, REACH, 16, LANES), BF),
            pltpu.VMEM((2, CH, REACH, 16, LANES), BF),
            pltpu.VMEM((CH, REACH, 16, LANES), BF),
            pltpu.VMEM((2, CH, REACH, 16, LANES), BF),
            pltpu.VMEM((2, CH, REACH, rows, student_width), BF),
            pltpu.VMEM((2, CH, REACH, rows, student_width), BF),
            pltpu.VMEM((2 + tokens // 16, 16, LANES), F32),
            pltpu.VMEM((tokens, student_width), F32),
            dma((7,)),
            dma((2,)),
            dma((2,)),
            dma((2, CH, REACH, HALVES)),
            dma((2, CH, REACH, HALVES)),
            dma((2, CH, REACH)),
            dma((2, CH, REACH)),
            dma((2, CH, REACH)),
            dma((2, CH, REACH)),
            dma((2, CH, REACH, PIECES)),
            dma((2, CH, REACH, PIECES)),
        ],
        compiler_params=pltpu.CompilerParams(
            collective_id=0, has_side_effects=True, vmem_limit_bytes=56 * 2**20
        ),
        cost_estimate=pl.CostEstimate(flops=2 * 10**9, bytes_accessed=10**7, transcendentals=3 * 10**6),
        name="banded_teacher",
    )(teacher_q, teacher_k, teacher_v, band, head_mix.T, latents, w_qk, w_v)


def solution(mesh):
    in_specs = (
        P("az", "tm", None),
        P("az", "tm", None),
        P("az", "tm", None),
        P("tm", "az"),
        P(),
        P("az", "tm", None),
        P(),
        P(),
    )
    out_specs = P("az", "tm", None)
    return jax.shard_map(shards, mesh=mesh, in_specs=in_specs, out_specs=out_specs, check_vma=False)
```

```python
import math

import jax
import jax.numpy as jnp
from jax import lax
from jax.experimental import pallas as pl
from jax.experimental.pallas import tpu as pltpu
from jax.sharding import PartitionSpec as P

MESH = pl.DeviceIdType.MESH
BF = jnp.bfloat16
F32 = jnp.float32
REACH = 4
SPLIT = (96, 32)
PIECE = (32, 16)
CH = len(SPLIT)
START = (0, 96)
PIECES = tuple(n // p for n, p in zip(SPLIT, PIECE))
PARTS = (4, 2)
LANES = 128


def normed(x):
    return x * lax.rsqrt(jnp.mean(x * x, axis=-1, keepdims=True) + 1e-06)


def kernel(
    q_hbm, k_hbm, v_hbm, band_ref, mix_ref, lat_hbm, wqk_hbm, wv_hbm, out_ref,
    q_in, k_in, v_in, lat, wqk, wv,
    qn0, qn1, kt, qbuf0, qbuf1, o0, o1, o_own, pp0, pp1, pp_own, tsnd, tbuf, rsnd, rbuf,
    msnd0, msnd1, mbuf0, mbuf1, abuf, town, fac, sout,
    in_sem, lat_s, lat_r, q_s, q_r, t_s, t_r, r_s, r_r, m_s, m_r, a_s, a_r,
):
    az = lax.axis_index("az")
    tm = lax.axis_index("tm")
    n_az = lax.axis_size("az")
    n_tm = lax.axis_size("tm")
    heads_s, heads_t = mix_ref.shape
    tokens = q_in.shape[0]
    qn, qbuf, o_ref, pp = (qn0, qn1), (qbuf0, qbuf1), (o0, o1), (pp0, pp1)
    msnd, mbuf = (msnd0, msnd1), (mbuf0, mbuf1)
    hd = LANES
    heads_in = [heads_t // n for n in PARTS]
    scale2 = math.log2(math.e) / math.sqrt(hd)

    def az_dev(by):
        return (lax.rem(az + by + n_az, n_az), tm)

    def tm_dev(by):
        return (az, lax.rem(tm + by + n_tm, n_tm))

    window = tokens // 2
    first = pl.ds(0, SPLIT[0])
    rest = pl.ds(SPLIT[0], SPLIT[1])
    loads = [
        pltpu.make_async_copy(q_hbm.at[0, first], q_in.at[first], in_sem.at[0]),
        pltpu.make_async_copy(k_hbm.at[0], k_in, in_sem.at[1]),
        pltpu.make_async_copy(lat_hbm.at[0], lat.at[pl.ds(window, tokens)], in_sem.at[2]),
        pltpu.make_async_copy(v_hbm.at[0], v_in, in_sem.at[3]),
        pltpu.make_async_copy(wqk_hbm, wqk, in_sem.at[4]),
        pltpu.make_async_copy(wv_hbm, wv, in_sem.at[5]),
        pltpu.make_async_copy(q_hbm.at[0, rest], q_in.at[rest], in_sem.at[6]),
    ]
    loads[0].start()
    to_right, to_left = tm < n_tm - 1, tm > 0

    @pl.when(tm == 0)
    def _():
        lat[0:window] = jnp.zeros((window, lat.shape[1]), BF)

    @pl.when(tm == n_tm - 1)
    def _():
        lat[tokens + window:] = jnp.zeros((window, lat.shape[1]), BF)


    barrier = pltpu.get_barrier_semaphore()
    for sign in (1, -1):
        pl.semaphore_signal(barrier, inc=1, device_id=az_dev(sign), device_id_type=MESH)
    for sign in (1, -1):
        pl.semaphore_signal(barrier, inc=1, device_id=tm_dev(sign), device_id_type=MESH)

    def remote(src, dst, send, recv, dev):
        return pltpu.make_async_remote_copy(
            src_ref=src, dst_ref=dst, send_sem=send, recv_sem=recv, device_id=dev, device_id_type=MESH
        )

    def q_copy(side, c, k, i):
        part = pl.ds(i * heads_in[c], heads_in[c])
        src = qn[c].at[part] if k == 1 else qbuf[c].at[side, k - 2, part]
        return remote(
            src, qbuf[c].at[side, k - 1, part],
            q_s.at[side, c, k - 1, i], q_r.at[side, c, k - 1, i], az_dev(1 - 2 * side),
        )

    def t_copy(side, c, k):
        return remote(
            tsnd.at[side, c, k - 1], tbuf.at[side, c, k - 1],
            t_s.at[side, c, k - 1], t_r.at[side, c, k - 1], az_dev((2 * side - 1) * k),
        )

    def r_copy(side, c, k):
        return remote(
            rsnd.at[c, k - 1], rbuf.at[side, c, k - 1],
            r_s.at[side, c, k - 1], r_r.at[side, c, k - 1], az_dev((1 - 2 * side) * k),
        )

    def a_copy(side):
        last = CH - 1
        return remote(
            tsnd.at[side, last, REACH - 1], abuf.at[1 - side], a_s.at[side], a_r.at[1 - side], az_dev(2 * REACH)
        )

    def m_copy(side, c, k, i):
        part = pl.ds(i * PIECE[c], PIECE[c])
        return remote(
            msnd[c].at[side, k - 1, part], mbuf[c].at[side, k - 1, part],
            m_s.at[side, c, k - 1, i], m_r.at[side, c, k - 1, i], az_dev(2 * side - 1),
        )

    def lat_copy(side):
        src = lat.at[pl.ds(window + (1 - side) * (tokens - window), window)]
        dst = lat.at[pl.ds(side * (tokens + window), window)]
        return remote(src, dst, lat_s.at[side], lat_r.at[side], tm_dev(1 - 2 * side))

    def norm_q(c, i):
        def one(j, _):
            h = i * heads_in[c] + j
            x = q_in[START[c]:START[c] + SPLIT[c], pl.ds(pl.multiple_of(h * hd, hd), hd)].astype(F32)
            qn[c][h] = normed(x).astype(BF)
            return 0
        lax.fori_loop(0, heads_in[c], one, 0, unroll=5)

    def norm_k(h, _):
        x = k_in[:, pl.ds(pl.multiple_of(h * hd, hd), hd)].astype(F32)
        kt[h] = normed(x).T.astype(BF)
        return 0

    def send_first(c, i):
        for side in (0, 1):
            q_copy(side, c, 1, i).start()

    loads[0].wait()
    for i in (1, 2, 6, 3, 4, 5):
        loads[i].start()
    norm_q(0, 0)
    pl.semaphore_wait(barrier, 4)
    send_first(0, 0)
    for i in range(1, PARTS[0]):
        norm_q(0, i)
    loads[1].wait()
    lax.fori_loop(0, heads_t // 2, norm_k, 0, unroll=5)
    send_first(0, 1)
    lax.fori_loop(heads_t // 2, heads_t, norm_k, 0, unroll=5)
    send_first(0, 2)
    loads[6].wait()
    for i in range(PARTS[1]):
        norm_q(1, i)
    loads[2].wait()
    pl.when(to_right)(lat_copy(0).start)
    pl.when(to_left)(lat_copy(1).start)
    loads[3].wait()
    send_first(0, 3)

    lane8 = lax.broadcasted_iota(jnp.int32, (8, LANES), 1)
    row8 = lax.broadcasted_iota(jnp.int32, (8, LANES), 0)

    def scores(left, right, dst, first, count, sums):
        lane = lax.broadcasted_iota(jnp.int32, sums.shape, 1)

        def group(i, sums):
            for j in range(5):
                h = first + i * 5 + j
                q = jnp.concatenate([left[h], right[h]], axis=0)
                s = jnp.dot(q, kt[h], preferred_element_type=F32)
                p = jnp.exp2(s * scale2)
                sums = jnp.where(lane == h, jnp.sum(p, axis=1, keepdims=True), sums)
                v = v_in[:, pl.ds(pl.multiple_of(h * hd, hd), hd)]
                dst[h] = jnp.dot(p.astype(BF), v, preferred_element_type=F32)
            return sums
        return lax.fori_loop(0, count // 5, group, sums)

    def roll(x, by):
        return pltpu.roll(x, by, 1)

    def lift(x):
        return pltpu.roll(x, 4, 0)

    def below(n, x, y):
        return jnp.where(lane8 < n, x, y)

    def by_head(x):
        if x.shape[0] < LANES:
            x = jnp.concatenate([x, jnp.zeros((LANES - x.shape[0], LANES), F32)], axis=0)
        t = x.T
        return t[0:8], t[8:16], t[16:24]

    def by_query(t0, t1, t2):
        return jnp.concatenate([t0, t1, t2, jnp.zeros((LANES - 24, LANES), F32)], axis=0).T

    def pack_large(t):
        t0, t1, t2 = t
        tail = jnp.where(row8 < 4, roll(t2, 96), lift(roll(t2, 64)))
        return jnp.concatenate([below(96, t0, tail), below(96, t1, roll(t2, 32))], axis=0)

    def unpack_large(x):
        m0, m1 = x[0:8], x[8:16]
        return m0, m1, below(32, roll(m0, 32), below(64, lift(roll(m0, 64)), roll(m1, 96)))

    def pack_small(t, at):
        def to(x, lanes):
            by = (lanes - at) % LANES
            return roll(x, by) if by else x
        m = below(32, to(t[0], 0), below(64, to(t[1], 32), to(t[2], 64)))
        return jnp.concatenate([m, jnp.zeros((8, LANES), F32)], axis=0)

    def unpack_small(x, at):
        m = x[0:8]

        def to(lanes):
            by = (at - lanes) % LANES
            return roll(m, by) if by else m
        return to(0), to(32), to(64)

    def pack(c, sums):
        n = SPLIT[c]
        if c == 0:
            return pack_large(by_head(sums[0:n])), pack_large(by_head(sums[n:2 * n]))
        t = by_head(sums)
        return pack_small(t, 0), pack_small(t, n)

    def unpack(c, left, right):
        n = SPLIT[c]
        if c == 0:
            return jnp.concatenate([by_query(*unpack_large(x))[0:n] for x in (left, right)], axis=0)
        both = zip(unpack_small(left, 0), unpack_small(right, n))
        return by_query(*[below(n, x, y) for x, y in both])[0:2 * n]

    def own_scores():
        sums = scores(qn[0], qn[1], o_own, 0, heads_t, jnp.zeros((tokens, LANES), F32))
        t = by_head(sums)
        town[0] = pack_large(t)
        town[1] = pack_small(t, START[1])

    def send_sums(c, k, sums):
        for side, t in enumerate(pack(c, sums)):
            tsnd[side, c, k - 1] = t.astype(BF)
            if c == CH - 1 and k == REACH:
                a_copy(side).start()
            t_copy(side, c, k).start()

    reach = band_ref[0, 0]

    def within(k):
        return jnp.where(k <= reach, 1.0, 0.0).astype(F32)

    def add_sums(c, total, ks):
        for k in ks:
            for side in (0, 1):
                t_copy(side, c, k).wait_recv()
                total = total + within(k) * tbuf[side, c, k - 1].astype(F32)
        return total

    def send_factors(c, k, value):
        rsnd[c, k - 1] = value.astype(BF)
        for side in (0, 1):
            r_copy(side, c, k).start()

    def gather_sums(c):
        inverse = 1.0 / add_sums(c, town[c], range(1, REACH + 1))
        town[c] = inverse
        for k in range(REACH, 0, -1):
            send_factors(c, k, within(k) * inverse)

    def gather_near():
        c = CH - 1
        total = add_sums(c, town[c], range(1, REACH))
        town[c] = total
        send_factors(c, REACH, jnp.where(jnp.full(total.shape, reach) >= REACH, total, jnp.inf))

    def gather_far():
        c = CH - 1
        inverse = 1.0 / add_sums(c, town[c], (REACH,))
        town[c] = inverse
        for k in range(REACH - 1, 0, -1):
            send_factors(c, k, within(k) * inverse)

    block = 32

    def mix_tile(o, dst, factors):
        n = factors.shape[0]
        fac[0:n] = factors

        def one(b, _):
            at = pl.ds(pl.multiple_of(b * block, block), block)
            f = fac[at]
            acc = [None] * heads_s
            for h in range(heads_t):
                x = o[h, at] * f[:, h:h + 1]
                for s in range(heads_s):
                    y = x * mix_ref[s, h]
                    acc[s] = y if acc[s] is None else acc[s] + y
            for s in range(heads_s):
                dst[at, s * hd:(s + 1) * hd] = acc[s]
            return 0
        lax.fori_loop(0, n // block, one, 0)

    def mix_remote(c, k):
        for side in (0, 1):
            r_copy(side, c, k).wait_recv()
        sent = [rbuf[side, c, k - 1].astype(F32) for side in (0, 1)]
        if c == CH - 1 and k == REACH:
            for side in (0, 1):
                a_copy(1 - side).wait_recv()
                sent[side] = 1.0 / (sent[side] + tsnd[side, c, k - 1].astype(F32) + abuf[side].astype(F32))
        factors = unpack(c, *sent)
        mix_tile(o_ref[c].at[k - 1], pp[c].at[k - 1], factors)

    def mix_own():
        large = unpack_large(town[0])
        small = unpack_small(town[1], START[1])
        mix_tile(o_own, pp_own, by_query(*[below(START[1], x, y) for x, y in zip(large, small)]))

    def pass_back(c, k, pieces=None):
        for i in range(PIECES[c]) if pieces is None else pieces:
            at = slice(i * PIECE[c], (i + 1) * PIECE[c])
            for side in (0, 1):
                share = side * SPLIT[c] + i * PIECE[c]
                part = pp[c][k - 1, share:share + PIECE[c]]
                if k < REACH:
                    m_copy(side, c, k + 1, i).wait_recv()
                    part = part + mbuf[c][side, k, at].astype(F32)
                msnd[c][side, k - 1, at] = part.astype(BF)
                m_copy(side, c, k, i).start()

    span = tokens + 2 * window

    def student(pair):
        cols = 2 * hd
        at = pl.multiple_of(pair * cols, cols)
        width = heads_s * hd
        sq = jnp.dot(lat[pl.ds(window, tokens)], wqk[:, pl.ds(at, cols)], preferred_element_type=F32)
        sk = jnp.dot(lat[...], wqk[:, pl.ds(pl.multiple_of(width + pair * cols, cols), cols)], preferred_element_type=F32)
        sv = jnp.dot(lat[...], wv[:, pl.ds(at, cols)], preferred_element_type=F32).astype(BF)
        pos_q = lax.broadcasted_iota(jnp.int32, (tokens, span), 0)
        pos_k = lax.broadcasted_iota(jnp.int32, (tokens, span), 1) - window
        at_k = pos_k + tm * tokens
        keep = (jnp.abs(pos_q - pos_k) <= window) & (at_k >= 0) & (at_k < n_tm * tokens)
        for j in range(2):
            part = slice(j * hd, (j + 1) * hd)
            snq = normed(sq[:, part]).astype(BF)
            snk = normed(sk[:, part]).astype(BF)
            s = lax.dot_general(snq, snk, (((1,), (1,)), ((), ())), preferred_element_type=F32)
            p = jnp.where(keep, jnp.exp2(s * scale2), 0.0)
            total = jnp.sum(p, axis=1, keepdims=True)
            o = jnp.dot(p.astype(BF), sv[:, part], preferred_element_type=F32)
            sout[:, pl.ds(pl.multiple_of(at + j * hd, hd), hd)] = o / total

    def arrive(c, k, i, sums):
        for side in (0, 1):
            q_copy(side, c, k, i).wait_recv()
            if k < REACH:
                q_copy(side, c, k + 1, i).start()
        if k == REACH and c + 1 < CH:
            for n in range(PARTS[c + 1]):
                if (n + 1) * PARTS[c] // PARTS[c + 1] - 1 == i:
                    send_first(c + 1, n)
        if sums is None:
            sums = jnp.zeros((2 * SPLIT[c], LANES), F32)
        return scores(qbuf[c].at[0, k - 1], qbuf[c].at[1, k - 1], o_ref[c].at[k - 1], i * heads_in[c], heads_in[c], sums)

    own_scores()
    for k in range(1, REACH + 1):
        sums = None
        for i in range(PARTS[0]):
            sums = arrive(0, k, i, sums)
            if k == 1 and i == 1:
                loads[4].wait()
                loads[5].wait()
                pl.when(to_left)(lat_copy(0).wait_recv)
                pl.when(to_right)(lat_copy(1).wait_recv)
            if i == 2:
                student(k - 1)
        send_sums(0, k, sums)

    for k in range(1, REACH + 1):
        sums = arrive(1, k, 0, None)
        if k == 2:
            gather_sums(0)
        sums = arrive(1, k, 1, sums)
        send_sums(1, k, sums)
        if k == 3:
            mix_remote(0, 4)
            pass_back(0, 4)
            mix_remote(0, 3)
    gather_near()
    pass_back(0, 3)
    gather_far()
    mix_remote(1, 4)
    pass_back(1, 4)
    mix_remote(0, 2)
    pass_back(0, 2)
    mix_remote(1, 3)
    pass_back(1, 3)
    mix_remote(0, 1)
    pass_back(0, 1)
    mix_remote(1, 2)
    pass_back(1, 2)
    mix_remote(1, 1)
    mix_own()
    pass_back(1, 1)

    for c in range(CH):
        for i in range(PIECES[c]):
            at = slice(START[c] + i * PIECE[c], START[c] + (i + 1) * PIECE[c])
            target = pp_own[at]
            for side in (0, 1):
                m_copy(side, c, 1, i).wait_recv()
                target = target + mbuf[c][side, 0, i * PIECE[c]:(i + 1) * PIECE[c]].astype(F32)
            out_ref[0, at] = sout[at] - target

    pl.when(to_right)(lat_copy(0).wait_send)
    pl.when(to_left)(lat_copy(1).wait_send)
    for side in (0, 1):
        a_copy(side).wait_send()
        for c in range(CH):
            for k in range(1, REACH + 1):
                for i in range(PARTS[c]):
                    q_copy(side, c, k, i).wait_send()
                t_copy(side, c, k).wait_send()
                r_copy(side, c, k).wait_send()
                for i in range(PIECES[c]):
                    m_copy(side, c, k, i).wait_send()


def shards(teacher_q, teacher_k, teacher_v, band, head_mix, latents, w_qk, w_v):
    tokens, width = teacher_q.shape[1:]
    heads_t, heads_s = head_mix.shape
    hd = width // heads_t
    student_width = latents.shape[2]
    dma = pltpu.SemaphoreType.DMA
    anywhere = pl.BlockSpec(memory_space=pl.ANY)
    scalars = pl.BlockSpec(memory_space=pltpu.SMEM)
    return pl.pallas_call(
        kernel,
        out_shape=pltpu.VMEM((1, tokens, student_width), F32),
        in_specs=[anywhere, anywhere, anywhere, scalars, scalars, anywhere, anywhere, anywhere],
        out_specs=pl.BlockSpec(memory_space=pltpu.VMEM),
        scratch_shapes=[
            pltpu.VMEM((tokens, width), BF),
            pltpu.VMEM((tokens, width), BF),
            pltpu.VMEM((tokens, width), BF),
            pltpu.VMEM((2 * tokens, student_width), BF),
            pltpu.VMEM(w_qk.shape, BF),
            pltpu.VMEM(w_v.shape, BF),
            *[pltpu.VMEM((heads_t, n, hd), BF) for n in SPLIT],
            pltpu.VMEM((heads_t, hd, tokens), BF),
            *[pltpu.VMEM((2, REACH, heads_t, n, hd), BF) for n in SPLIT],
            *[pltpu.VMEM((REACH, heads_t, 2 * n, hd), F32) for n in SPLIT],
            pltpu.VMEM((heads_t, tokens, hd), F32),
            *[pltpu.VMEM((REACH, 2 * n, student_width), F32) for n in SPLIT],
            pltpu.VMEM((tokens, student_width), F32),
            pltpu.VMEM((2, CH, REACH, 16, LANES), BF),
            pltpu.VMEM((2, CH, REACH, 16, LANES), BF),
            pltpu.VMEM((CH, REACH, 16, LANES), BF),
            pltpu.VMEM((2, CH, REACH, 16, LANES), BF),
            *[pltpu.VMEM((2, REACH, n, student_width), BF) for n in SPLIT],
            *[pltpu.VMEM((2, REACH, n, student_width), BF) for n in SPLIT],
            pltpu.VMEM((2, 16, LANES), BF),
            pltpu.VMEM((CH, 16, LANES), F32),
            pltpu.VMEM((2 * max(SPLIT), LANES), F32),
            pltpu.VMEM((tokens, student_width), F32),
            dma((7,)),
            dma((2,)),
            dma((2,)),
            dma((2, CH, REACH, max(PARTS))),
            dma((2, CH, REACH, max(PARTS))),
            dma((2, CH, REACH)),
            dma((2, CH, REACH)),
            dma((2, CH, REACH)),
            dma((2, CH, REACH)),
            dma((2, CH, REACH, max(PIECES))),
            dma((2, CH, REACH, max(PIECES))),
            dma((2,)),
            dma((2,)),
        ],
        compiler_params=pltpu.CompilerParams(
            collective_id=0, has_side_effects=True, vmem_limit_bytes=56 * 2**20
        ),
        cost_estimate=pl.CostEstimate(flops=2 * 10**9, bytes_accessed=10**7, transcendentals=3 * 10**6),
        name="banded_teacher",
    )(teacher_q, teacher_k, teacher_v, band, head_mix.T, latents, w_qk, w_v)


def solution(mesh):
    in_specs = (
        P("az", "tm", None),
        P("az", "tm", None),
        P("az", "tm", None),
        P("tm", "az"),
        P(),
        P("az", "tm", None),
        P(),
        P(),
    )
    out_specs = P("az", "tm", None)
    return jax.shard_map(shards, mesh=mesh, in_specs=in_specs, out_specs=out_specs, check_vma=False)
```

```python
import math

import jax
import jax.numpy as jnp
from jax import lax
from jax.experimental import pallas as pl
from jax.experimental.pallas import tpu as pltpu
from jax.sharding import PartitionSpec as P

MESH = pl.DeviceIdType.MESH
BF = jnp.bfloat16
F32 = jnp.float32
REACH = 4
SPLIT = (96, 32)
PIECE = (32, 16)
CH = len(SPLIT)
START = (0, 96)
PIECES = tuple(n // p for n, p in zip(SPLIT, PIECE))
PARTS = (4, 2)
LANES = 128


def normed(x):
    return x * lax.rsqrt(jnp.mean(x * x, axis=-1, keepdims=True) + 1e-06)


def kernel(
    q_hbm, k_hbm, v_hbm, band_ref, mix_ref, lat_hbm, wqk_hbm, wv_hbm, out_ref,
    q_in, k_in, v_in, lat, wqk, wv,
    qn0, qn1, kt, qbuf0, qbuf1, o0, o1, o_own, pp0, pp1, pp_own, tsnd, tbuf, rsnd, rbuf,
    msnd0, msnd1, mbuf0, mbuf1, abuf, town, fac, sout,
    in_sem, lat_s, lat_r, q_s, q_r, t_s, t_r, r_s, r_r, m_s, m_r, a_s, a_r,
):
    az = lax.axis_index("az")
    tm = lax.axis_index("tm")
    n_az = lax.axis_size("az")
    n_tm = lax.axis_size("tm")
    heads_s, heads_t = mix_ref.shape
    tokens = q_in.shape[0]
    qn, qbuf, o_ref, pp = (qn0, qn1), (qbuf0, qbuf1), (o0, o1), (pp0, pp1)
    msnd, mbuf = (msnd0, msnd1), (mbuf0, mbuf1)
    hd = LANES
    heads_in = [heads_t // n for n in PARTS]
    scale2 = math.log2(math.e) / math.sqrt(hd)

    def az_dev(by):
        return (lax.rem(az + by + n_az, n_az), tm)

    def tm_dev(by):
        return (az, lax.rem(tm + by + n_tm, n_tm))

    window = tokens // 2
    first = pl.ds(0, SPLIT[0])
    rest = pl.ds(SPLIT[0], SPLIT[1])
    loads = [
        pltpu.make_async_copy(q_hbm.at[0, first], q_in.at[first], in_sem.at[0]),
        pltpu.make_async_copy(k_hbm.at[0], k_in, in_sem.at[1]),
        pltpu.make_async_copy(lat_hbm.at[0], lat.at[pl.ds(window, tokens)], in_sem.at[2]),
        pltpu.make_async_copy(v_hbm.at[0], v_in, in_sem.at[3]),
        pltpu.make_async_copy(wqk_hbm, wqk, in_sem.at[4]),
        pltpu.make_async_copy(wv_hbm, wv, in_sem.at[5]),
        pltpu.make_async_copy(q_hbm.at[0, rest], q_in.at[rest], in_sem.at[6]),
    ]
    loads[0].start()
    to_right, to_left = tm < n_tm - 1, tm > 0

    @pl.when(tm == 0)
    def _():
        lat[0:window] = jnp.zeros((window, lat.shape[1]), BF)

    @pl.when(tm == n_tm - 1)
    def _():
        lat[tokens + window:] = jnp.zeros((window, lat.shape[1]), BF)


    barrier = pltpu.get_barrier_semaphore()
    for sign in (1, -1):
        pl.semaphore_signal(barrier, inc=1, device_id=az_dev(sign), device_id_type=MESH)
    for sign, there in ((1, to_right), (-1, to_left)):
        @pl.when(there)
        def _(sign=sign):
            pl.semaphore_signal(barrier, inc=1, device_id=tm_dev(sign), device_id_type=MESH)

    def remote(src, dst, send, recv, dev):
        return pltpu.make_async_remote_copy(
            src_ref=src, dst_ref=dst, send_sem=send, recv_sem=recv, device_id=dev, device_id_type=MESH
        )

    def q_copy(side, c, k, i):
        part = pl.ds(i * heads_in[c], heads_in[c])
        src = qn[c].at[part] if k == 1 else qbuf[c].at[side, k - 2, part]
        return remote(
            src, qbuf[c].at[side, k - 1, part],
            q_s.at[side, c, k - 1, i], q_r.at[side, c, k - 1, i], az_dev(1 - 2 * side),
        )

    def t_copy(side, c, k):
        return remote(
            tsnd.at[side, c, k - 1], tbuf.at[side, c, k - 1],
            t_s.at[side, c, k - 1], t_r.at[side, c, k - 1], az_dev((2 * side - 1) * k),
        )

    def r_copy(side, c, k):
        return remote(
            rsnd.at[c, k - 1], rbuf.at[side, c, k - 1],
            r_s.at[side, c, k - 1], r_r.at[side, c, k - 1], az_dev((1 - 2 * side) * k),
        )

    def a_copy(side):
        last = CH - 1
        return remote(
            tsnd.at[side, last, REACH - 1], abuf.at[1 - side], a_s.at[side], a_r.at[1 - side], az_dev(2 * REACH)
        )

    def m_copy(side, c, k, i):
        part = pl.ds(i * PIECE[c], PIECE[c])
        return remote(
            msnd[c].at[side, k - 1, part], mbuf[c].at[side, k - 1, part],
            m_s.at[side, c, k - 1, i], m_r.at[side, c, k - 1, i], az_dev(2 * side - 1),
        )

    def lat_copy(side):
        src = lat.at[pl.ds(window + (1 - side) * (tokens - window), window)]
        dst = lat.at[pl.ds(side * (tokens + window), window)]
        return remote(src, dst, lat_s.at[side], lat_r.at[side], tm_dev(1 - 2 * side))

    def norm_q(c, i):
        def one(j, _):
            h = i * heads_in[c] + j
            x = q_in[START[c]:START[c] + SPLIT[c], pl.ds(pl.multiple_of(h * hd, hd), hd)].astype(F32)
            qn[c][h] = normed(x).astype(BF)
            return 0
        lax.fori_loop(0, heads_in[c], one, 0, unroll=5)

    def norm_k(h, _):
        x = k_in[:, pl.ds(pl.multiple_of(h * hd, hd), hd)].astype(F32)
        kt[h] = normed(x).T.astype(BF)
        return 0

    def send_first(c, i):
        for side in (0, 1):
            q_copy(side, c, 1, i).start()

    loads[0].wait()
    for i in (1, 2, 6, 3, 4, 5):
        loads[i].start()
    norm_q(0, 0)
    pl.semaphore_wait(barrier, 2 + lax.min(tm, 1) + lax.min(n_tm - 1 - tm, 1))
    send_first(0, 0)
    for i in range(1, PARTS[0]):
        norm_q(0, i)
    loads[1].wait()
    lax.fori_loop(0, heads_t // 2, norm_k, 0, unroll=5)
    send_first(0, 1)
    lax.fori_loop(heads_t // 2, heads_t, norm_k, 0, unroll=5)
    send_first(0, 2)
    loads[6].wait()
    for i in range(PARTS[1]):
        norm_q(1, i)
    loads[2].wait()
    pl.when(to_right)(lat_copy(0).start)
    pl.when(to_left)(lat_copy(1).start)
    loads[3].wait()
    send_first(0, 3)

    lane8 = lax.broadcasted_iota(jnp.int32, (8, LANES), 1)
    row8 = lax.broadcasted_iota(jnp.int32, (8, LANES), 0)

    def scores(left, right, dst, first, count, sums):
        lane = lax.broadcasted_iota(jnp.int32, sums.shape, 1)

        def group(i, sums):
            for j in range(5):
                h = first + i * 5 + j
                q = jnp.concatenate([left[h], right[h]], axis=0)
                s = jnp.dot(q, kt[h], preferred_element_type=F32)
                p = jnp.exp2(s * scale2)
                sums = jnp.where(lane == h, jnp.sum(p, axis=1, keepdims=True), sums)
                v = v_in[:, pl.ds(pl.multiple_of(h * hd, hd), hd)]
                dst[h] = jnp.dot(p.astype(BF), v, preferred_element_type=F32)
            return sums
        return lax.fori_loop(0, count // 5, group, sums)

    def roll(x, by):
        return pltpu.roll(x, by, 1)

    def lift(x):
        return pltpu.roll(x, 4, 0)

    def below(n, x, y):
        return jnp.where(lane8 < n, x, y)

    def by_head(x):
        if x.shape[0] < LANES:
            x = jnp.concatenate([x, jnp.zeros((LANES - x.shape[0], LANES), F32)], axis=0)
        t = x.T
        return t[0:8], t[8:16], t[16:24]

    def by_query(t0, t1, t2):
        return jnp.concatenate([t0, t1, t2, jnp.zeros((LANES - 24, LANES), F32)], axis=0).T

    def pack_large(t):
        t0, t1, t2 = t
        tail = jnp.where(row8 < 4, roll(t2, 96), lift(roll(t2, 64)))
        return jnp.concatenate([below(96, t0, tail), below(96, t1, roll(t2, 32))], axis=0)

    def unpack_large(x):
        m0, m1 = x[0:8], x[8:16]
        return m0, m1, below(32, roll(m0, 32), below(64, lift(roll(m0, 64)), roll(m1, 96)))

    def pack_small(t, at):
        def to(x, lanes):
            by = (lanes - at) % LANES
            return roll(x, by) if by else x
        m = below(32, to(t[0], 0), below(64, to(t[1], 32), to(t[2], 64)))
        return jnp.concatenate([m, jnp.zeros((8, LANES), F32)], axis=0)

    def unpack_small(x, at):
        m = x[0:8]

        def to(lanes):
            by = (at - lanes) % LANES
            return roll(m, by) if by else m
        return to(0), to(32), to(64)

    def pack(c, sums):
        n = SPLIT[c]
        if c == 0:
            return pack_large(by_head(sums[0:n])), pack_large(by_head(sums[n:2 * n]))
        t = by_head(sums)
        return pack_small(t, 0), pack_small(t, n)

    def unpack(c, left, right):
        n = SPLIT[c]
        if c == 0:
            return jnp.concatenate([by_query(*unpack_large(x))[0:n] for x in (left, right)], axis=0)
        both = zip(unpack_small(left, 0), unpack_small(right, n))
        return by_query(*[below(n, x, y) for x, y in both])[0:2 * n]

    def own_scores():
        sums = scores(qn[0], qn[1], o_own, 0, heads_t, jnp.zeros((tokens, LANES), F32))
        t = by_head(sums)
        town[0] = pack_large(t)
        town[1] = pack_small(t, START[1])

    def send_sums(c, k, sums):
        for side, t in enumerate(pack(c, sums)):
            tsnd[side, c, k - 1] = t.astype(BF)
            if c == CH - 1 and k == REACH:
                a_copy(side).start()
            t_copy(side, c, k).start()

    reach = band_ref[0, 0]

    def within(k):
        return jnp.where(k <= reach, 1.0, 0.0).astype(F32)

    def add_sums(c, total, ks):
        for k in ks:
            for side in (0, 1):
                t_copy(side, c, k).wait_recv()
                total = total + within(k) * tbuf[side, c, k - 1].astype(F32)
        return total

    def send_factors(c, k, value):
        rsnd[c, k - 1] = value.astype(BF)
        for side in (0, 1):
            r_copy(side, c, k).start()

    def gather_sums(c):
        inverse = 1.0 / add_sums(c, town[c], range(1, REACH + 1))
        town[c] = inverse
        for k in range(REACH, 0, -1):
            send_factors(c, k, within(k) * inverse)

    def gather_near():
        c = CH - 1
        total = add_sums(c, town[c], range(1, REACH))
        town[c] = total
        send_factors(c, REACH, jnp.where(jnp.full(total.shape, reach) >= REACH, total, jnp.inf))

    def gather_far():
        c = CH - 1
        inverse = 1.0 / add_sums(c, town[c], (REACH,))
        town[c] = inverse
        for k in range(REACH - 1, 0, -1):
            send_factors(c, k, within(k) * inverse)

    block = 32

    def mix_tile(o, dst, factors):
        n = factors.shape[0]
        fac[0:n] = factors

        def one(b, _):
            at = pl.ds(pl.multiple_of(b * block, block), block)
            f = fac[at]
            acc = [None] * heads_s
            for h in range(heads_t):
                x = o[h, at] * f[:, h:h + 1]
                for s in range(heads_s):
                    y = x * mix_ref[s, h]
                    acc[s] = y if acc[s] is None else acc[s] + y
            for s in range(heads_s):
                dst[at, s * hd:(s + 1) * hd] = acc[s]
            return 0
        lax.fori_loop(0, n // block, one, 0)

    def mix_remote(c, k):
        for side in (0, 1):
            r_copy(side, c, k).wait_recv()
        sent = [rbuf[side, c, k - 1].astype(F32) for side in (0, 1)]
        if c == CH - 1 and k == REACH:
            for side in (0, 1):
                a_copy(1 - side).wait_recv()
                sent[side] = 1.0 / (sent[side] + tsnd[side, c, k - 1].astype(F32) + abuf[side].astype(F32))
        factors = unpack(c, *sent)
        mix_tile(o_ref[c].at[k - 1], pp[c].at[k - 1], factors)

    def mix_own():
        large = unpack_large(town[0])
        small = unpack_small(town[1], START[1])
        mix_tile(o_own, pp_own, by_query(*[below(START[1], x, y) for x, y in zip(large, small)]))

    def pass_back(c, k, pieces=None):
        for i in range(PIECES[c]) if pieces is None else pieces:
            at = slice(i * PIECE[c], (i + 1) * PIECE[c])
            for side in (0, 1):
                share = side * SPLIT[c] + i * PIECE[c]
                part = pp[c][k - 1, share:share + PIECE[c]]
                if k < REACH:
                    m_copy(side, c, k + 1, i).wait_recv()
                    part = part + mbuf[c][side, k, at].astype(F32)
                msnd[c][side, k - 1, at] = part.astype(BF)
                m_copy(side, c, k, i).start()

    span = tokens + 2 * window

    def student(pair):
        cols = 2 * hd
        at = pl.multiple_of(pair * cols, cols)
        width = heads_s * hd
        sq = jnp.dot(lat[pl.ds(window, tokens)], wqk[:, pl.ds(at, cols)], preferred_element_type=F32)
        sk = jnp.dot(lat[...], wqk[:, pl.ds(pl.multiple_of(width + pair * cols, cols), cols)], preferred_element_type=F32)
        sv = jnp.dot(lat[...], wv[:, pl.ds(at, cols)], preferred_element_type=F32).astype(BF)
        pos_q = lax.broadcasted_iota(jnp.int32, (tokens, span), 0)
        pos_k = lax.broadcasted_iota(jnp.int32, (tokens, span), 1) - window
        at_k = pos_k + tm * tokens
        keep = (jnp.abs(pos_q - pos_k) <= window) & (at_k >= 0) & (at_k < n_tm * tokens)
        for j in range(2):
            part = slice(j * hd, (j + 1) * hd)
            snq = normed(sq[:, part]).astype(BF)
            snk = normed(sk[:, part]).astype(BF)
            s = lax.dot_general(snq, snk, (((1,), (1,)), ((), ())), preferred_element_type=F32)
            p = jnp.where(keep, jnp.exp2(s * scale2), 0.0)
            total = jnp.sum(p, axis=1, keepdims=True)
            o = jnp.dot(p.astype(BF), sv[:, part], preferred_element_type=F32)
            sout[:, pl.ds(pl.multiple_of(at + j * hd, hd), hd)] = o / total

    def arrive(c, k, i, sums):
        for side in (0, 1):
            q_copy(side, c, k, i).wait_recv()
            if k < REACH:
                q_copy(side, c, k + 1, i).start()
        if k == REACH and c + 1 < CH:
            for n in range(PARTS[c + 1]):
                if (n + 1) * PARTS[c] // PARTS[c + 1] - 1 == i:
                    send_first(c + 1, n)
        if sums is None:
            sums = jnp.zeros((2 * SPLIT[c], LANES), F32)
        return scores(qbuf[c].at[0, k - 1], qbuf[c].at[1, k - 1], o_ref[c].at[k - 1], i * heads_in[c], heads_in[c], sums)

    own_scores()
    for k in range(1, REACH + 1):
        sums = None
        for i in range(PARTS[0]):
            sums = arrive(0, k, i, sums)
            if k == 1 and i == 1:
                loads[4].wait()
                loads[5].wait()
                pl.when(to_left)(lat_copy(0).wait_recv)
                pl.when(to_right)(lat_copy(1).wait_recv)
            if i == 2:
                student(k - 1)
        send_sums(0, k, sums)

    for k in range(1, REACH + 1):
        sums = arrive(1, k, 0, None)
        if k == 2:
            gather_sums(0)
        sums = arrive(1, k, 1, sums)
        send_sums(1, k, sums)
        if k == 3:
            mix_remote(0, 4)
            pass_back(0, 4)
            mix_remote(0, 3)
    gather_near()
    pass_back(0, 3)
    gather_far()
    mix_remote(1, 4)
    pass_back(1, 4)
    mix_remote(0, 2)
    pass_back(0, 2)
    mix_remote(1, 3)
    pass_back(1, 3)
    mix_remote(0, 1)
    mix_remote(1, 2)
    pass_back(0, 1, (0,))
    pass_back(1, 2)
    pass_back(0, 1, (1, 2))
    mix_remote(1, 1)
    mix_own()
    pass_back(1, 1)

    pl.when(to_right)(lat_copy(0).wait_send)
    pl.when(to_left)(lat_copy(1).wait_send)
    for side in (0, 1):
        a_copy(side).wait_send()
        for c in range(CH):
            for k in range(1, REACH + 1):
                for i in range(PARTS[c]):
                    q_copy(side, c, k, i).wait_send()
                t_copy(side, c, k).wait_send()
                r_copy(side, c, k).wait_send()
                if k > 1:
                    for i in range(PIECES[c]):
                        m_copy(side, c, k, i).wait_send()

    for c in range(CH):
        for i in range(PIECES[c]):
            at = slice(START[c] + i * PIECE[c], START[c] + (i + 1) * PIECE[c])
            target = pp_own[at]
            for side in (0, 1):
                m_copy(side, c, 1, i).wait_recv()
                target = target + mbuf[c][side, 0, i * PIECE[c]:(i + 1) * PIECE[c]].astype(F32)
            out_ref[0, at] = sout[at] - target

    for side in (0, 1):
        for c in range(CH):
            for i in range(PIECES[c]):
                m_copy(side, c, 1, i).wait_send()


def shards(teacher_q, teacher_k, teacher_v, band, head_mix, latents, w_qk, w_v):
    tokens, width = teacher_q.shape[1:]
    heads_t, heads_s = head_mix.shape
    hd = width // heads_t
    student_width = latents.shape[2]
    dma = pltpu.SemaphoreType.DMA
    anywhere = pl.BlockSpec(memory_space=pl.ANY)
    scalars = pl.BlockSpec(memory_space=pltpu.SMEM)
    return pl.pallas_call(
        kernel,
        out_shape=pltpu.VMEM((1, tokens, student_width), F32),
        in_specs=[anywhere, anywhere, anywhere, scalars, scalars, anywhere, anywhere, anywhere],
        out_specs=pl.BlockSpec(memory_space=pltpu.VMEM),
        scratch_shapes=[
            pltpu.VMEM((tokens, width), BF),
            pltpu.VMEM((tokens, width), BF),
            pltpu.VMEM((tokens, width), BF),
            pltpu.VMEM((2 * tokens, student_width), BF),
            pltpu.VMEM(w_qk.shape, BF),
            pltpu.VMEM(w_v.shape, BF),
            *[pltpu.VMEM((heads_t, n, hd), BF) for n in SPLIT],
            pltpu.VMEM((heads_t, hd, tokens), BF),
            *[pltpu.VMEM((2, REACH, heads_t, n, hd), BF) for n in SPLIT],
            *[pltpu.VMEM((REACH, heads_t, 2 * n, hd), F32) for n in SPLIT],
            pltpu.VMEM((heads_t, tokens, hd), F32),
            *[pltpu.VMEM((REACH, 2 * n, student_width), F32) for n in SPLIT],
            pltpu.VMEM((tokens, student_width), F32),
            pltpu.VMEM((2, CH, REACH, 16, LANES), BF),
            pltpu.VMEM((2, CH, REACH, 16, LANES), BF),
            pltpu.VMEM((CH, REACH, 16, LANES), BF),
            pltpu.VMEM((2, CH, REACH, 16, LANES), BF),
            *[pltpu.VMEM((2, REACH, n, student_width), BF) for n in SPLIT],
            *[pltpu.VMEM((2, REACH, n, student_width), BF) for n in SPLIT],
            pltpu.VMEM((2, 16, LANES), BF),
            pltpu.VMEM((CH, 16, LANES), F32),
            pltpu.VMEM((2 * max(SPLIT), LANES), F32),
            pltpu.VMEM((tokens, student_width), F32),
            dma((7,)),
            dma((2,)),
            dma((2,)),
            dma((2, CH, REACH, max(PARTS))),
            dma((2, CH, REACH, max(PARTS))),
            dma((2, CH, REACH)),
            dma((2, CH, REACH)),
            dma((2, CH, REACH)),
            dma((2, CH, REACH)),
            dma((2, CH, REACH, max(PIECES))),
            dma((2, CH, REACH, max(PIECES))),
            dma((2,)),
            dma((2,)),
        ],
        compiler_params=pltpu.CompilerParams(
            collective_id=0, has_side_effects=True, vmem_limit_bytes=56 * 2**20
        ),
        cost_estimate=pl.CostEstimate(flops=2 * 10**9, bytes_accessed=10**7, transcendentals=3 * 10**6),
        name="banded_teacher",
    )(teacher_q, teacher_k, teacher_v, band, head_mix.T, latents, w_qk, w_v)


def solution(mesh):
    in_specs = (
        P("az", "tm", None),
        P("az", "tm", None),
        P("az", "tm", None),
        P("tm", "az"),
        P(),
        P("az", "tm", None),
        P(),
        P(),
    )
    out_specs = P("az", "tm", None)
    return jax.shard_map(shards, mesh=mesh, in_specs=in_specs, out_specs=out_specs, check_vma=False)
```

```python
import math

import jax
import jax.numpy as jnp
from jax import lax
from jax.experimental import pallas as pl
from jax.experimental.pallas import tpu as pltpu
from jax.sharding import PartitionSpec as P

MESH = pl.DeviceIdType.MESH
BF = jnp.bfloat16
F32 = jnp.float32
REACH = 4
SPLIT = (96, 32)
PIECE = (48, 16)
CH = len(SPLIT)
START = (0, 96)
PIECES = tuple(n // p for n, p in zip(SPLIT, PIECE))
PARTS = (4, 2)
LANES = 128


def normed(x):
    return x * lax.rsqrt(jnp.mean(x * x, axis=-1, keepdims=True) + 1e-06)


def kernel(
    q_hbm, k_hbm, v_hbm, band_ref, mix_ref, lat_hbm, wqk_hbm, wv_hbm, out_ref,
    q_in, k_in, v_in, lat, wqk, wv,
    qn0, qn1, kt, qbuf0, qbuf1, o0, o1, o_own, pp0, pp1, pp_own, tsnd, tbuf, rsnd, rbuf,
    msnd0, msnd1, mbuf0, mbuf1, abuf, town, fac, sout,
    in_sem, lat_s, lat_r, q_s, q_r, t_s, t_r, r_s, r_r, m_s, m_r, a_s, a_r,
):
    az = lax.axis_index("az")
    tm = lax.axis_index("tm")
    n_az = lax.axis_size("az")
    n_tm = lax.axis_size("tm")
    heads_s, heads_t = mix_ref.shape
    tokens = q_in.shape[0]
    qn, qbuf, o_ref, pp = (qn0, qn1), (qbuf0, qbuf1), (o0, o1), (pp0, pp1)
    msnd, mbuf = (msnd0, msnd1), (mbuf0, mbuf1)
    hd = LANES
    heads_in = [heads_t // n for n in PARTS]
    scale2 = math.log2(math.e) / math.sqrt(hd)

    def az_dev(by):
        return (lax.rem(az + by + n_az, n_az), tm)

    def tm_dev(by):
        return (az, lax.rem(tm + by + n_tm, n_tm))

    window = tokens // 2
    first = pl.ds(0, SPLIT[0])
    rest = pl.ds(SPLIT[0], SPLIT[1])
    loads = [
        pltpu.make_async_copy(q_hbm.at[0, first], q_in.at[first], in_sem.at[0]),
        pltpu.make_async_copy(k_hbm.at[0], k_in, in_sem.at[1]),
        pltpu.make_async_copy(lat_hbm.at[0], lat.at[pl.ds(window, tokens)], in_sem.at[2]),
        pltpu.make_async_copy(v_hbm.at[0], v_in, in_sem.at[3]),
        pltpu.make_async_copy(wqk_hbm, wqk, in_sem.at[4]),
        pltpu.make_async_copy(wv_hbm, wv, in_sem.at[5]),
        pltpu.make_async_copy(q_hbm.at[0, rest], q_in.at[rest], in_sem.at[6]),
    ]
    loads[0].start()
    to_right, to_left = tm < n_tm - 1, tm > 0

    @pl.when(tm == 0)
    def _():
        lat[0:window] = jnp.zeros((window, lat.shape[1]), BF)

    @pl.when(tm == n_tm - 1)
    def _():
        lat[tokens + window:] = jnp.zeros((window, lat.shape[1]), BF)


    barrier = pltpu.get_barrier_semaphore()
    for sign in (1, -1):
        pl.semaphore_signal(barrier, inc=1, device_id=az_dev(sign), device_id_type=MESH)
    for sign, there in ((1, to_right), (-1, to_left)):
        @pl.when(there)
        def _(sign=sign):
            pl.semaphore_signal(barrier, inc=1, device_id=tm_dev(sign), device_id_type=MESH)

    def remote(src, dst, send, recv, dev):
        return pltpu.make_async_remote_copy(
            src_ref=src, dst_ref=dst, send_sem=send, recv_sem=recv, device_id=dev, device_id_type=MESH
        )

    def q_copy(side, c, k, i):
        part = pl.ds(i * heads_in[c], heads_in[c])
        src = qn[c].at[part] if k == 1 else qbuf[c].at[side, k - 2, part]
        return remote(
            src, qbuf[c].at[side, k - 1, part],
            q_s.at[side, c, k - 1, i], q_r.at[side, c, k - 1, i], az_dev(1 - 2 * side),
        )

    def t_copy(side, c, k):
        return remote(
            tsnd.at[side, c, k - 1], tbuf.at[side, c, k - 1],
            t_s.at[side, c, k - 1], t_r.at[side, c, k - 1], az_dev((2 * side - 1) * k),
        )

    def r_copy(side, c, k):
        return remote(
            rsnd.at[c, k - 1], rbuf.at[side, c, k - 1],
            r_s.at[side, c, k - 1], r_r.at[side, c, k - 1], az_dev((1 - 2 * side) * k),
        )

    def a_copy(side):
        last = CH - 1
        return remote(
            tsnd.at[side, last, REACH - 1], abuf.at[1 - side], a_s.at[side], a_r.at[1 - side], az_dev(2 * REACH)
        )

    def m_copy(side, c, k, i):
        part = pl.ds(i * PIECE[c], PIECE[c])
        return remote(
            msnd[c].at[side, k - 1, part], mbuf[c].at[side, k - 1, part],
            m_s.at[side, c, k - 1, i], m_r.at[side, c, k - 1, i], az_dev(2 * side - 1),
        )

    def lat_copy(side):
        src = lat.at[pl.ds(window + (1 - side) * (tokens - window), window)]
        dst = lat.at[pl.ds(side * (tokens + window), window)]
        return remote(src, dst, lat_s.at[side], lat_r.at[side], tm_dev(1 - 2 * side))

    def norm_q(c, i):
        def one(j, _):
            h = i * heads_in[c] + j
            x = q_in[START[c]:START[c] + SPLIT[c], pl.ds(pl.multiple_of(h * hd, hd), hd)].astype(F32)
            qn[c][h] = normed(x).astype(BF)
            return 0
        lax.fori_loop(0, heads_in[c], one, 0, unroll=5)

    def norm_k(h, _):
        x = k_in[:, pl.ds(pl.multiple_of(h * hd, hd), hd)].astype(F32)
        kt[h] = normed(x).T.astype(BF)
        return 0

    def send_first(c, i):
        for side in (0, 1):
            q_copy(side, c, 1, i).start()

    loads[0].wait()
    for i in (1, 2, 6, 3, 4, 5):
        loads[i].start()
    norm_q(0, 0)
    pl.semaphore_wait(barrier, 2 + lax.min(tm, 1) + lax.min(n_tm - 1 - tm, 1))
    send_first(0, 0)
    for i in range(1, PARTS[0]):
        norm_q(0, i)
    loads[1].wait()
    lax.fori_loop(0, heads_t // 2, norm_k, 0, unroll=5)
    send_first(0, 1)
    lax.fori_loop(heads_t // 2, heads_t, norm_k, 0, unroll=5)
    send_first(0, 2)
    loads[6].wait()
    for i in range(PARTS[1]):
        norm_q(1, i)
    loads[2].wait()
    pl.when(to_right)(lat_copy(0).start)
    pl.when(to_left)(lat_copy(1).start)
    loads[3].wait()
    send_first(0, 3)

    lane8 = lax.broadcasted_iota(jnp.int32, (8, LANES), 1)
    row8 = lax.broadcasted_iota(jnp.int32, (8, LANES), 0)

    def scores(left, right, dst, first, count, sums):
        lane = lax.broadcasted_iota(jnp.int32, sums.shape, 1)

        def group(i, sums):
            for j in range(5):
                h = first + i * 5 + j
                q = jnp.concatenate([left[h], right[h]], axis=0)
                s = jnp.dot(q, kt[h], preferred_element_type=F32)
                p = jnp.exp2(s * scale2)
                sums = jnp.where(lane == h, jnp.sum(p, axis=1, keepdims=True), sums)
                v = v_in[:, pl.ds(pl.multiple_of(h * hd, hd), hd)]
                dst[h] = jnp.dot(p.astype(BF), v, preferred_element_type=F32)
            return sums
        return lax.fori_loop(0, count // 5, group, sums)

    def roll(x, by):
        return pltpu.roll(x, by, 1)

    def lift(x):
        return pltpu.roll(x, 4, 0)

    def below(n, x, y):
        return jnp.where(lane8 < n, x, y)

    def by_head(x):
        if x.shape[0] < LANES:
            x = jnp.concatenate([x, jnp.zeros((LANES - x.shape[0], LANES), F32)], axis=0)
        t = x.T
        return t[0:8], t[8:16], t[16:24]

    def by_query(t0, t1, t2):
        return jnp.concatenate([t0, t1, t2, jnp.zeros((LANES - 24, LANES), F32)], axis=0).T

    def pack_large(t):
        t0, t1, t2 = t
        tail = jnp.where(row8 < 4, roll(t2, 96), lift(roll(t2, 64)))
        return jnp.concatenate([below(96, t0, tail), below(96, t1, roll(t2, 32))], axis=0)

    def unpack_large(x):
        m0, m1 = x[0:8], x[8:16]
        return m0, m1, below(32, roll(m0, 32), below(64, lift(roll(m0, 64)), roll(m1, 96)))

    def pack_small(t, at):
        def to(x, lanes):
            by = (lanes - at) % LANES
            return roll(x, by) if by else x
        m = below(32, to(t[0], 0), below(64, to(t[1], 32), to(t[2], 64)))
        return jnp.concatenate([m, jnp.zeros((8, LANES), F32)], axis=0)

    def unpack_small(x, at):
        m = x[0:8]

        def to(lanes):
            by = (at - lanes) % LANES
            return roll(m, by) if by else m
        return to(0), to(32), to(64)

    def pack(c, sums):
        n = SPLIT[c]
        if c == 0:
            return pack_large(by_head(sums[0:n])), pack_large(by_head(sums[n:2 * n]))
        t = by_head(sums)
        return pack_small(t, 0), pack_small(t, n)

    def unpack(c, left, right):
        n = SPLIT[c]
        if c == 0:
            return jnp.concatenate([by_query(*unpack_large(x))[0:n] for x in (left, right)], axis=0)
        both = zip(unpack_small(left, 0), unpack_small(right, n))
        return by_query(*[below(n, x, y) for x, y in both])[0:2 * n]

    def own_scores():
        sums = scores(qn[0], qn[1], o_own, 0, heads_t, jnp.zeros((tokens, LANES), F32))
        t = by_head(sums)
        town[0] = pack_large(t)
        town[1] = pack_small(t, START[1])

    def send_sums(c, k, sums):
        for side, t in enumerate(pack(c, sums)):
            tsnd[side, c, k - 1] = t.astype(BF)
            if c == CH - 1 and k == REACH:
                a_copy(side).start()
            t_copy(side, c, k).start()

    reach = band_ref[0, 0]

    def within(k):
        return jnp.where(k <= reach, 1.0, 0.0).astype(F32)

    def add_sums(c, total, ks):
        for k in ks:
            for side in (0, 1):
                t_copy(side, c, k).wait_recv()
                total = total + within(k) * tbuf[side, c, k - 1].astype(F32)
        return total

    def send_factors(c, k, value):
        rsnd[c, k - 1] = value.astype(BF)
        for side in (0, 1):
            r_copy(side, c, k).start()

    def gather_sums(c):
        inverse = 1.0 / add_sums(c, town[c], range(1, REACH + 1))
        town[c] = inverse
        for k in range(REACH, 0, -1):
            send_factors(c, k, within(k) * inverse)

    def gather_near():
        c = CH - 1
        total = add_sums(c, town[c], range(1, REACH))
        town[c] = total
        send_factors(c, REACH, jnp.where(jnp.full(total.shape, reach) >= REACH, total, jnp.inf))

    def gather_far():
        c = CH - 1
        inverse = 1.0 / add_sums(c, town[c], (REACH,))
        town[c] = inverse
        for k in range(REACH - 1, 0, -1):
            send_factors(c, k, within(k) * inverse)

    block = 32

    def mix_tile(o, dst, factors):
        n = factors.shape[0]
        fac[0:n] = factors

        def one(b, _):
            at = pl.ds(pl.multiple_of(b * block, block), block)
            f = fac[at]
            acc = [None] * heads_s
            for h in range(heads_t):
                x = o[h, at] * f[:, h:h + 1]
                for s in range(heads_s):
                    y = x * mix_ref[s, h]
                    acc[s] = y if acc[s] is None else acc[s] + y
            for s in range(heads_s):
                dst[at, s * hd:(s + 1) * hd] = acc[s]
            return 0
        lax.fori_loop(0, n // block, one, 0)

    def mix_remote(c, k):
        for side in (0, 1):
            r_copy(side, c, k).wait_recv()
        sent = [rbuf[side, c, k - 1].astype(F32) for side in (0, 1)]
        if c == CH - 1 and k == REACH:
            for side in (0, 1):
                a_copy(1 - side).wait_recv()
                sent[side] = 1.0 / (sent[side] + tsnd[side, c, k - 1].astype(F32) + abuf[side].astype(F32))
        factors = unpack(c, *sent)
        mix_tile(o_ref[c].at[k - 1], pp[c].at[k - 1], factors)

    def mix_own():
        large = unpack_large(town[0])
        small = unpack_small(town[1], START[1])
        mix_tile(o_own, pp_own, by_query(*[below(START[1], x, y) for x, y in zip(large, small)]))

    def pass_back(c, k, pieces=None):
        for i in range(PIECES[c]) if pieces is None else pieces:
            at = slice(i * PIECE[c], (i + 1) * PIECE[c])
            for side in (0, 1):
                share = side * SPLIT[c] + i * PIECE[c]
                part = pp[c][k - 1, share:share + PIECE[c]]
                if k < REACH:
                    m_copy(side, c, k + 1, i).wait_recv()
                    part = part + mbuf[c][side, k, at].astype(F32)
                msnd[c][side, k - 1, at] = part.astype(BF)
                m_copy(side, c, k, i).start()

    span = tokens + 2 * window

    def student(pair):
        cols = 2 * hd
        at = pl.multiple_of(pair * cols, cols)
        width = heads_s * hd
        sq = jnp.dot(lat[pl.ds(window, tokens)], wqk[:, pl.ds(at, cols)], preferred_element_type=F32)
        sk = jnp.dot(lat[...], wqk[:, pl.ds(pl.multiple_of(width + pair * cols, cols), cols)], preferred_element_type=F32)
        sv = jnp.dot(lat[...], wv[:, pl.ds(at, cols)], preferred_element_type=F32).astype(BF)
        pos_q = lax.broadcasted_iota(jnp.int32, (tokens, span), 0)
        pos_k = lax.broadcasted_iota(jnp.int32, (tokens, span), 1) - window
        at_k = pos_k + tm * tokens
        keep = (jnp.abs(pos_q - pos_k) <= window) & (at_k >= 0) & (at_k < n_tm * tokens)
        for j in range(2):
            part = slice(j * hd, (j + 1) * hd)
            snq = normed(sq[:, part]).astype(BF)
            snk = normed(sk[:, part]).astype(BF)
            s = lax.dot_general(snq, snk, (((1,), (1,)), ((), ())), preferred_element_type=F32)
            p = jnp.where(keep, jnp.exp2(s * scale2), 0.0)
            total = jnp.sum(p, axis=1, keepdims=True)
            o = jnp.dot(p.astype(BF), sv[:, part], preferred_element_type=F32)
            sout[:, pl.ds(pl.multiple_of(at + j * hd, hd), hd)] = o / total

    def arrive(c, k, i, sums):
        for side in (0, 1):
            q_copy(side, c, k, i).wait_recv()
            if k < REACH:
                q_copy(side, c, k + 1, i).start()
        if k == REACH and c + 1 < CH:
            for n in range(PARTS[c + 1]):
                if (n + 1) * PARTS[c] // PARTS[c + 1] - 1 == i:
                    send_first(c + 1, n)
        if sums is None:
            sums = jnp.zeros((2 * SPLIT[c], LANES), F32)
        return scores(qbuf[c].at[0, k - 1], qbuf[c].at[1, k - 1], o_ref[c].at[k - 1], i * heads_in[c], heads_in[c], sums)

    own_scores()
    for k in range(1, REACH + 1):
        sums = None
        for i in range(PARTS[0]):
            sums = arrive(0, k, i, sums)
            if k == 1 and i == 1:
                loads[4].wait()
                loads[5].wait()
                pl.when(to_left)(lat_copy(0).wait_recv)
                pl.when(to_right)(lat_copy(1).wait_recv)
            if i == 2:
                student(k - 1)
        send_sums(0, k, sums)

    for k in range(1, REACH + 1):
        sums = arrive(1, k, 0, None)
        if k == 2:
            gather_sums(0)
        sums = arrive(1, k, 1, sums)
        send_sums(1, k, sums)
        if k == 3:
            mix_remote(0, 4)
            pass_back(0, 4)
            mix_remote(0, 3)
    gather_near()
    pass_back(0, 3)
    gather_far()
    mix_remote(1, 4)
    pass_back(1, 4)
    mix_remote(0, 2)
    pass_back(0, 2)
    mix_remote(1, 3)
    pass_back(1, 3)
    mix_remote(0, 1)
    mix_remote(1, 2)
    pass_back(0, 1, (0,))
    pass_back(1, 2)
    pass_back(0, 1, (1,))
    mix_remote(1, 1)
    mix_own()
    pass_back(1, 1)

    pl.when(to_right)(lat_copy(0).wait_send)
    pl.when(to_left)(lat_copy(1).wait_send)
    for side in (0, 1):
        a_copy(side).wait_send()
        for c in range(CH):
            for k in range(1, REACH + 1):
                for i in range(PARTS[c]):
                    q_copy(side, c, k, i).wait_send()
                t_copy(side, c, k).wait_send()
                r_copy(side, c, k).wait_send()
                if k > 1:
                    for i in range(PIECES[c]):
                        m_copy(side, c, k, i).wait_send()

    for c in range(CH):
        for i in range(PIECES[c]):
            at = slice(START[c] + i * PIECE[c], START[c] + (i + 1) * PIECE[c])
            target = pp_own[at]
            for side in (0, 1):
                m_copy(side, c, 1, i).wait_recv()
                target = target + mbuf[c][side, 0, i * PIECE[c]:(i + 1) * PIECE[c]].astype(F32)
            out_ref[0, at] = sout[at] - target

    for side in (0, 1):
        for c in range(CH):
            for i in range(PIECES[c]):
                m_copy(side, c, 1, i).wait_send()


def shards(teacher_q, teacher_k, teacher_v, band, head_mix, latents, w_qk, w_v):
    tokens, width = teacher_q.shape[1:]
    heads_t, heads_s = head_mix.shape
    hd = width // heads_t
    student_width = latents.shape[2]
    dma = pltpu.SemaphoreType.DMA
    anywhere = pl.BlockSpec(memory_space=pl.ANY)
    scalars = pl.BlockSpec(memory_space=pltpu.SMEM)
    return pl.pallas_call(
        kernel,
        out_shape=pltpu.VMEM((1, tokens, student_width), F32),
        in_specs=[anywhere, anywhere, anywhere, scalars, scalars, anywhere, anywhere, anywhere],
        out_specs=pl.BlockSpec(memory_space=pltpu.VMEM),
        scratch_shapes=[
            pltpu.VMEM((tokens, width), BF),
            pltpu.VMEM((tokens, width), BF),
            pltpu.VMEM((tokens, width), BF),
            pltpu.VMEM((2 * tokens, student_width), BF),
            pltpu.VMEM(w_qk.shape, BF),
            pltpu.VMEM(w_v.shape, BF),
            *[pltpu.VMEM((heads_t, n, hd), BF) for n in SPLIT],
            pltpu.VMEM((heads_t, hd, tokens), BF),
            *[pltpu.VMEM((2, REACH, heads_t, n, hd), BF) for n in SPLIT],
            *[pltpu.VMEM((REACH, heads_t, 2 * n, hd), F32) for n in SPLIT],
            pltpu.VMEM((heads_t, tokens, hd), F32),
            *[pltpu.VMEM((REACH, 2 * n, student_width), F32) for n in SPLIT],
            pltpu.VMEM((tokens, student_width), F32),
            pltpu.VMEM((2, CH, REACH, 16, LANES), BF),
            pltpu.VMEM((2, CH, REACH, 16, LANES), BF),
            pltpu.VMEM((CH, REACH, 16, LANES), BF),
            pltpu.VMEM((2, CH, REACH, 16, LANES), BF),
            *[pltpu.VMEM((2, REACH, n, student_width), BF) for n in SPLIT],
            *[pltpu.VMEM((2, REACH, n, student_width), BF) for n in SPLIT],
            pltpu.VMEM((2, 16, LANES), BF),
            pltpu.VMEM((CH, 16, LANES), F32),
            pltpu.VMEM((2 * max(SPLIT), LANES), F32),
            pltpu.VMEM((tokens, student_width), F32),
            dma((7,)),
            dma((2,)),
            dma((2,)),
            dma((2, CH, REACH, max(PARTS))),
            dma((2, CH, REACH, max(PARTS))),
            dma((2, CH, REACH)),
            dma((2, CH, REACH)),
            dma((2, CH, REACH)),
            dma((2, CH, REACH)),
            dma((2, CH, REACH, max(PIECES))),
            dma((2, CH, REACH, max(PIECES))),
            dma((2,)),
            dma((2,)),
        ],
        compiler_params=pltpu.CompilerParams(
            collective_id=0, has_side_effects=True, vmem_limit_bytes=56 * 2**20
        ),
        cost_estimate=pl.CostEstimate(flops=2 * 10**9, bytes_accessed=10**7, transcendentals=3 * 10**6),
        name="banded_teacher",
    )(teacher_q, teacher_k, teacher_v, band, head_mix.T, latents, w_qk, w_v)


def solution(mesh):
    in_specs = (
        P("az", "tm", None),
        P("az", "tm", None),
        P("az", "tm", None),
        P("tm", "az"),
        P(),
        P("az", "tm", None),
        P(),
        P(),
    )
    out_specs = P("az", "tm", None)
    return jax.shard_map(shards, mesh=mesh, in_specs=in_specs, out_specs=out_specs, check_vma=False)
```
